32 devices in a mesh: seq: 8 (over y, x, core), head: 4 (over z).
Axes of the slice: x: 2, y: 2, z: 4, core: 2. Of those that a mesh axis runs over, the one named last changes fastest.
Arguments:
- query_rows: bfloat16 [4096, 4096], P('seq', 'head'), may hold values from -6 to 6
- key_rows: bfloat16 [4096, 4096], P('seq', 'head'), may hold values from -6 to 6
- value_rows: bfloat16 [4096, 4096], P('seq', 'head'), may hold values from -6 to 6
- out_weight: bfloat16 [4096, 4096], P('seq', 'head'), may hold values from -0.09375 to 0.09375
- target_rows: bfloat16 [4096, 4096], P('seq', 'head'), may hold values from -6 to 6
Outputs:
- output: bfloat16 [4096, 4096], P('seq', 'head')
- grad_query: bfloat16 [4096, 4096], P('seq', 'head')
- grad_key: bfloat16 [4096, 4096], P('seq', 'head')
- grad_value: bfloat16 [4096, 4096], P('seq', 'head')
- grad_weight: float32 [4096, 4096], P('seq', 'head')
The draws below stay inside these ranges and needn't reach their ends.
All inputs are finite; a program needn't handle non-finite values.
Results may differ from the reference program's by a relative error of at most 0.019.
Values may be sent and summed in bfloat16 or wider, within the bound.
No kernel may reach another device: no remote copies, remote signals or barrier semaphores. Data moves between devices by JAX's collectives and lax.ppermute only.
A program may use at most 64 MiB of HBM per device.

```python
import math
import jax
import jax.numpy as jnp
from jax import lax

D = 4096
H = 32
DH = 128
BLK = 512
TOKENS = 4096
N_HEAD = 4


def spiked(values, own_key, source, target, shards_of, factor):
    owner, partner = [(jnp.arange(values.shape[axis_at]) // (values.shape[axis_at] // shards_of)).reshape([-1 if axis == axis_at else 1 for axis in range(values.ndim)]) for axis_at in (source, target)]
    chosen = jax.random.permutation(own_key, shards_of)[partner]
    strong = (owner == chosen) | (owner == (partner + shards_of // 2) % shards_of)
    return jnp.where(strong, factor * values, values)


def steps_of(rng, shape, shards, low, largest):
    level = 1.0
    for dim, parts in shards:
        steps = jax.random.uniform(jax.random.fold_in(jax.random.fold_in(rng, 6), dim), (parts,), jnp.float32, low / len(shards), largest / len(shards))
        level = level * jnp.repeat(jnp.exp(steps), shape[dim] // parts).reshape((-1,) + (1,) * (len(shape) - 1 - dim))
    return level


def normal_values(rng, shape, width, most, split=(), kind=jnp.bfloat16):
    factor_of = steps_of(rng, shape, split, -0.22, 0.18) if split else 1.0
    result = jax.random.normal(rng, shape, jnp.float32) * width * factor_of
    return jnp.minimum(jnp.maximum(result, -most), most).astype(kind)


def noise_with(key, shape, spread, most, pieces, heavy, held_as=jnp.bfloat16):
    result = spread * jax.random.normal(key, shape, jnp.float32)
    if pieces:
        result = result * steps_of(key, shape, pieces, -0.22, 0.18)
    return jnp.clip(spiked(result, jax.random.fold_in(key, 3), *heavy), -most, most).astype(held_as)


def setup_inputs(seed: int = 0) -> dict:
    key_of = jax.random.split(jax.random.key(seed), 6)
    query_rows = normal_values(key_of[0], (TOKENS, H * DH), 1.0, 6.0, ((0, 8), (1, 4)))
    key_rows = normal_values(key_of[1], (TOKENS, H * DH), 1.0, 6.0, ((0, 8), (1, 4)))
    value_rows = normal_values(key_of[2], (TOKENS, H * DH), 1.0, 6.0, ((0, 8), (1, 4)))
    out_weight = normal_values(key_of[3], (D, H * DH), (H * DH) ** -0.5, 0.09375, ((0, 8), (1, 4)))
    target_rows = noise_with(key_of[4], (TOKENS, D), 1.0, 6.0, ((0, 8), (1, 4)), (0, 1, 8, 2.0))
    return {"query_rows": query_rows, "key_rows": key_rows, "value_rows": value_rows, "out_weight": out_weight, "target_rows": target_rows}


EXACT = lax.Precision.HIGHEST

def reference(query_rows, key_rows, value_rows, out_weight, target_rows):
    block_count = TOKENS // BLK
    positions = jnp.arange(TOKENS, dtype=jnp.float32) + 1.0
    query_scale = lax.rsqrt(jnp.float32(DH) * positions)
    scaled = (query_rows.astype(jnp.float32) * query_scale[:, None]).astype(jnp.bfloat16)
    shaped = (block_count, BLK, H, DH)
    query_blocks = scaled.reshape(shaped)
    key_blocks = key_rows.reshape(shaped)
    value_blocks = value_rows.reshape(shaped)
    causal = jnp.tril(jnp.ones((BLK, BLK), dtype=bool))

    def forward_step(running, inputs):
        queries = inputs[0].astype(jnp.float32)
        keys_now = inputs[1].astype(jnp.float32)
        values_now = inputs[2].astype(jnp.float32)
        inter = jnp.einsum('thd,hde->the', queries, running, precision=EXACT)
        scores = jnp.einsum('thd,shd->hts', queries, keys_now)
        scores = jnp.where(causal, scores, 0.0).astype(jnp.bfloat16)
        intra = jnp.einsum('hts,she->the', scores.astype(jnp.float32), values_now)
        attended_now = (inter + intra).astype(jnp.bfloat16)
        update = jnp.einsum('shd,she->hde', keys_now, values_now)
        return (running + update, (attended_now, running))
    start_state = jnp.zeros((H, DH, DH), jnp.float32)
    final_state, (attended, before) = lax.scan(forward_step, start_state, (query_blocks, key_blocks, value_blocks))
    attended = attended.reshape(TOKENS, H * DH)
    group_width = H * DH // N_HEAD
    grouped_acts = attended.reshape(TOKENS, N_HEAD, group_width).transpose(1, 0, 2)
    grouped_weight = out_weight.reshape(D, N_HEAD, group_width).transpose(1, 0, 2)

    def add_group(running, inputs):
        partial_sum = lax.dot_general(inputs[0], inputs[1], (((1,), (1,)), ((), ())), preferred_element_type=jnp.float32)
        rounded = lax.optimization_barrier(partial_sum.astype(jnp.bfloat16))
        return (running + rounded.astype(jnp.float32), None)
    summed, unused = lax.scan(add_group, jnp.zeros((TOKENS, D), jnp.float32), (grouped_acts, grouped_weight))
    output = summed.astype(jnp.bfloat16)
    residual = (output.astype(jnp.float32) - target_rows.astype(jnp.float32)).astype(jnp.bfloat16)
    grad_attended = jnp.dot(residual, out_weight, preferred_element_type=jnp.float32).astype(jnp.bfloat16)
    grad_weight = lax.dot_general(residual, attended, (((0,), (0,)), ((), ())), preferred_element_type=jnp.float32) * (1.0 / math.sqrt(TOKENS))
    grad_blocks = grad_attended.reshape(shaped)

    def backward_step(running, inputs):
        queries = inputs[0].astype(jnp.float32)
        keys_now = inputs[1].astype(jnp.float32)
        values_now = inputs[2].astype(jnp.float32)
        grads_now = inputs[3].astype(jnp.float32)
        state_now = inputs[4]
        mixed = jnp.einsum('the,she->hts', grads_now, values_now)
        mixed = jnp.where(causal, mixed, 0.0).astype(jnp.bfloat16).astype(jnp.float32)
        scores = jnp.einsum('thd,shd->hts', queries, keys_now)
        scores = jnp.where(causal, scores, 0.0).astype(jnp.bfloat16).astype(jnp.float32)
        grad_scaled = jnp.einsum('the,hde->thd', grads_now, state_now, precision=EXACT)
        grad_scaled = grad_scaled + jnp.einsum('hts,shd->thd', mixed, keys_now)
        key_grad = jnp.einsum('she,hde->shd', values_now, running, precision=EXACT) + jnp.einsum('hts,thd->shd', mixed, queries)
        value_grad = jnp.einsum('shd,hde->she', keys_now, running, precision=EXACT) + jnp.einsum('hts,the->she', scores, grads_now)
        update = jnp.einsum('thd,the->hde', queries, grads_now)
        return (running + update, (grad_scaled, key_grad.astype(jnp.bfloat16), value_grad.astype(jnp.bfloat16)))
    final_grad, (grad_scaled, grad_key, grad_value) = lax.scan(backward_step, start_state, (query_blocks, key_blocks, value_blocks, grad_blocks, before), reverse=True)
    grad_query = (grad_scaled.reshape(TOKENS, H * DH) * query_scale[:, None]).astype(jnp.bfloat16)
    return (output, grad_query, grad_key.reshape(TOKENS, H * DH), grad_value.reshape(TOKENS, H * DH), grad_weight)
```

```python
import functools
import math

import jax
import jax.numpy as jnp
from jax import lax
from jax.experimental import pallas as pl
from jax.experimental.pallas import tpu as pltpu
from jax.sharding import PartitionSpec as P

DH = 128
CHUNKS = 2
F32 = jnp.float32
BF16 = jnp.bfloat16
VMEM_LIMIT = 16 * 1024 * 1024

NT = (((1,), (1,)), ((), ()))
TN = (((0,), (0,)), ((), ()))
NN = (((1,), (0,)), ((), ()))


def dot(a, b, dims):
    return lax.dot_general(a, b, dims, preferred_element_type=F32)


def split_dot(a, state, dims):
    high = state.astype(BF16)
    low = (state - high.astype(F32)).astype(BF16)
    return dot(a, high, dims) + dot(a, low, dims)


def causal_mask(rows):
    t = lax.broadcasted_iota(jnp.int32, (rows, rows), 0)
    s = lax.broadcasted_iota(jnp.int32, (rows, rows), 1)
    return s <= t


def outer_kernel(a_ref, b_ref, out_ref):
    out_ref[0] = dot(a_ref[...], b_ref[...], TN)


def forward_kernel(q_ref, k_ref, v_ref, scale_ref, scaled_ref, intra_ref):
    scaled = (q_ref[...].astype(F32) * scale_ref[...]).astype(BF16)
    scaled_ref[...] = scaled
    scores = dot(scaled, k_ref[...], NT)
    scores = jnp.where(causal_mask(scores.shape[0]), scores, 0.0).astype(BF16)
    intra_ref[...] = dot(scores, v_ref[...], NN)


def attended_kernel(scaled_ref, intra_ref, state_ref, out_ref):
    inter = split_dot(scaled_ref[...], state_ref[0], NN)
    out_ref[...] = (inter + intra_ref[...]).astype(BF16)


def backward_kernel(
    scaled_ref, k_ref, v_ref, g_ref, scale_ref, state_ref, dq_ref, dk_ref, dv_ref
):
    scaled, keys, values, grads = scaled_ref[...], k_ref[...], v_ref[...], g_ref[...]
    mask = causal_mask(scaled.shape[0])
    mixed = jnp.where(mask, dot(grads, values, NT), 0.0).astype(BF16)
    dq = split_dot(grads, state_ref[0], NT) + dot(mixed, keys, NN)
    dq_ref[...] = (dq * scale_ref[...]).astype(BF16)
    dk_ref[...] = dot(mixed, scaled, TN)
    scores = jnp.where(mask, dot(scaled, keys, NT), 0.0).astype(BF16)
    dv_ref[...] = dot(scores, grads, TN)


def finish_kernel(k_ref, v_ref, dk_part_ref, dv_part_ref, after_ref, dk_ref, dv_ref):
    after = after_ref[0]
    dk_ref[...] = (split_dot(v_ref[...], after, NT) + dk_part_ref[...]).astype(BF16)
    dv_ref[...] = (split_dot(k_ref[...], after, NN) + dv_part_ref[...]).astype(BF16)


def per_head(kernel, rows, heads, ins, outs, macs):
    specs = {
        "h": pl.BlockSpec((rows, DH), lambda h: (0, h)),
        "m": pl.BlockSpec((1, DH, DH), lambda h: (h, 0, 0)),
        "s": pl.BlockSpec((rows, 1), lambda h: (0, 0)),
    }
    shapes = {"h": (rows, heads * DH), "m": (heads, DH, DH)}
    return pl.pallas_call(
        kernel,
        grid=(heads,),
        in_specs=[specs[kind] for kind in ins],
        out_specs=[specs[kind] for kind, unused in outs],
        out_shape=[jax.ShapeDtypeStruct(shapes[kind], dtype) for kind, dtype in outs],
        compiler_params=pltpu.CompilerParams(vmem_limit_bytes=VMEM_LIMIT),
        cost_estimate=pl.CostEstimate(
            flops=2 * macs * heads,
            bytes_accessed=rows * heads * DH * 2 * (len(ins) + len(outs)),
            transcendentals=0,
        ),
    )


def core_swap(value):
    count = lax.axis_size("seq")
    return lax.ppermute(value, "seq", [(j, j ^ 1) for j in range(count)])


def chip_swap(value, delta):
    count = lax.axis_size("seq")
    return lax.ppermute(value, "seq", [(j, j ^ (2 * delta)) for j in range(count)])


def line_permutes(active):
    even = [pair for pair in active if min(pair) % 2 == 0]
    odd = [pair for pair in active if min(pair) % 2 == 1]
    return even, odd


def line_step(values, active):
    return [
        lax.ppermute(value, "head", pairs) if pairs else None
        for value, pairs in zip(values, line_permutes(active))
    ]


def line_sum(part_for):
    count = lax.axis_size("head")
    mine = lax.axis_index("head")
    got = [None, None]
    for step in range(1, count):
        active = [(j, j + 1) for j in range(count - 1) if j <= step - 1]
        active += [(j, j - 1) for j in range(1, count) if count - 1 - j <= step - 1]
        values = []
        for parity, pairs in enumerate(line_permutes(active)):
            if not pairs:
                values.append(None)
                continue
            target = jnp.where(mine % 2 == parity, mine + count - step, mine - count + step)
            value = part_for(jnp.clip(target, 0, count - 1))
            if got[1 - parity] is not None:
                value = (value.astype(F32) + got[1 - parity].astype(F32)).astype(BF16)
            values.append(value)
        got = line_step(values, active)
    total = part_for(mine).astype(F32)
    for value in got:
        if value is not None:
            total = total + value.astype(F32)
    return total


def line_gather(value):
    count = lax.axis_size("head")
    mine = lax.axis_index("head")
    zero = jnp.zeros_like(value)
    up, down = {}, {}
    got = [None, None]
    first = None
    for step in range(1, count):
        active = [(j, j + 1) for j in range(count - 1) if j >= step - 1]
        active += [(j, j - 1) for j in range(1, count) if j + step - 1 <= count - 1]
        values = [
            value if step == 1 else (zero if got[1 - parity] is None else got[1 - parity])
            for parity in (0, 1)
        ]
        got = line_step(values, active)
        if first is None:
            first = [item for item in got if item is not None]
        even, odd = [zero if item is None else item for item in got]
        up[step] = jnp.where(mine % 2 == 1, even, odd)
        down[step] = jnp.where(mine % 2 == 0, even, odd)
    pieces = [value]
    for back in range(1, count):
        pieces.append(jnp.where(mine >= back, up[back], down[count - back]))
    return pieces, first


def earlier_or_later(total, lower):
    position = lax.axis_index("seq")
    chips = lax.axis_size("seq") // 2
    chip, core = position // 2, position % 2
    half_heads = total.shape[0] // 2
    mine = total.astype(BF16)
    other = core_swap(mine)
    both = (mine.astype(F32) + other.astype(F32)).astype(BF16)
    half = lax.dynamic_slice_in_dim(both, core * half_heads, half_heads, 0)
    summed = jnp.zeros(half.shape, F32)
    for delta in range(1, chips):
        partner = chip ^ delta
        counts = (partner < chip) if lower else (partner > chip)
        summed = summed + jnp.where(counts, chip_swap(half, delta).astype(F32), 0.0)
    summed = summed.astype(BF16)
    swapped = core_swap(summed)
    first = jnp.where(core == 0, summed, swapped)
    second = jnp.where(core == 0, swapped, summed)
    whole = jnp.concatenate([first, second], axis=0).astype(F32)
    return whole + jnp.where(core == (1 if lower else 0), other.astype(F32), 0.0)


def on_device(query_rows, key_rows, value_rows, out_weight, target_rows):
    rows, width = query_rows.shape
    heads = width // DH
    groups = lax.axis_size("head")
    seq_count = lax.axis_size("seq")
    chips = seq_count // 2
    share = chips // groups
    position = lax.axis_index("seq")
    chip, core = position // 2, position % 2
    mine = lax.axis_index("head")
    held = out_weight.shape[0]
    part = held // CHUNKS
    call = functools.partial(per_head, rows=rows, heads=heads)

    weight_parts = []
    for c in range(CHUNKS):
        own = out_weight[c * part : (c + 1) * part]
        if c:
            own, unused = lax.optimization_barrier((own, weight_parts[-1]))
        pieces = [own] + [chip_swap(own, delta) for delta in range(1, chips)]
        weight_parts.append(jnp.concatenate(pieces, axis=0))

    positions = (position * rows + jnp.arange(rows, dtype=jnp.int32) + 1).astype(F32)
    scale = lax.rsqrt(F32(DH) * positions)[:, None]
    (key_value,) = call(outer_kernel, ins="hh", outs=[("m", F32)], macs=rows * DH * DH)(
        key_rows, value_rows
    )
    before = earlier_or_later(key_value, True)
    scaled, intra = call(
        forward_kernel, ins="hhhs", outs=[("h", BF16), ("h", F32)], macs=2 * rows * rows * DH
    )(query_rows, key_rows, value_rows, scale)
    (attended,) = call(attended_kernel, ins="hhm", outs=[("h", BF16)], macs=2 * rows * DH * DH)(
        scaled, intra, before
    )
    both_attended = jnp.concatenate([attended, core_swap(attended)], axis=0)

    targets = target_rows.reshape(rows, share, 2, held)
    own_target = lax.dynamic_index_in_dim(targets, core, 2, keepdims=False)
    sent_target = lax.dynamic_index_in_dim(targets, 1 - core, 2, keepdims=False)
    both_targets = jnp.concatenate([own_target, core_swap(sent_target)], axis=0)

    def columns_for(array, group):
        pieces = [
            lax.dynamic_slice_in_dim(array, ((group * share + j) ^ chip) * part, part, 1)
            for j in range(share)
        ]
        return pieces[0] if share == 1 else jnp.concatenate(pieces, axis=1)

    outputs = []
    residuals = []
    gate = None
    for c in range(CHUNKS):
        partial_out = dot(both_attended, weight_parts[c], NT).astype(BF16)
        if gate is not None:
            partial_out, *gate = lax.optimization_barrier((partial_out, *gate))
        summed = line_sum(functools.partial(columns_for, partial_out)).astype(BF16)
        target = both_targets[:, :, c * part : (c + 1) * part].reshape(2 * rows, share * part)
        residual = (summed.astype(F32) - target.astype(F32)).astype(BF16)
        pieces, gate = line_gather(residual)
        stacked = jnp.stack(pieces)
        ordered = []
        for delta in range(chips):
            piece_chip = chip ^ delta
            back = lax.rem(mine - piece_chip // share + groups, groups)
            piece = lax.dynamic_index_in_dim(stacked, back, 0, keepdims=False)
            ordered.append(
                lax.dynamic_slice_in_dim(piece, (piece_chip % share) * part, part, 1)
                if share > 1
                else piece
            )
        residuals.append(jnp.concatenate(ordered, axis=1))
        own_output = summed[:rows].reshape(rows, share, part)
        other_output = core_swap(summed[rows:]).reshape(rows, share, part)
        first = jnp.where(core == 0, own_output, other_output)
        second = jnp.where(core == 0, other_output, own_output)
        outputs.append(jnp.stack([first, second], axis=2))
    output = jnp.concatenate(outputs, axis=3).reshape(rows, width)

    weight_factor = 1.0 / math.sqrt(rows * seq_count)
    grad_both = jnp.zeros((2 * rows, width), F32)
    grad_weights = []
    for c in range(CHUNKS):
        grad_both = grad_both + dot(residuals[c], weight_parts[c], NN)
        product = (dot(residuals[c], both_attended, TN) * weight_factor).astype(BF16)
        total = product[:part].astype(F32)
        for delta in range(1, chips):
            piece = product[delta * part : (delta + 1) * part]
            total = total + chip_swap(piece, delta).astype(F32)
        grad_weights.append(total)
    grad_weight = jnp.concatenate(grad_weights, axis=0)
    swapped_grad = core_swap(grad_both[rows:].astype(BF16))
    grad_attended = (grad_both[:rows] + swapped_grad.astype(F32)).astype(BF16)

    (query_grad,) = call(outer_kernel, ins="hh", outs=[("m", F32)], macs=rows * DH * DH)(
        scaled, grad_attended
    )
    after = earlier_or_later(query_grad, False)
    grad_query, key_part, value_part = call(
        backward_kernel,
        ins="hhhhsm",
        outs=[("h", BF16), ("h", F32), ("h", F32)],
        macs=5 * rows * rows * DH,
    )(scaled, key_rows, value_rows, grad_attended, scale, before)
    grad_key, grad_value = call(
        finish_kernel, ins="hhhhm", outs=[("h", BF16), ("h", BF16)], macs=4 * rows * DH * DH
    )(key_rows, value_rows, key_part, value_part, after)
    return output, grad_query, grad_key, grad_value, grad_weight


def solution(mesh):
    placed = P("seq", "head")
    return jax.shard_map(
        on_device,
        mesh=mesh,
        in_specs=(placed,) * 5,
        out_specs=(placed,) * 5,
        check_vma=False,
    )
```

```python
import functools
import math

import jax
import jax.numpy as jnp
from jax import lax
from jax.experimental import pallas as pl
from jax.experimental.pallas import tpu as pltpu
from jax.sharding import PartitionSpec as P

DH = 128
CHUNKS = 2
F32 = jnp.float32
BF16 = jnp.bfloat16
VMEM_LIMIT = 16 * 1024 * 1024

NT = (((1,), (1,)), ((), ()))
TN = (((0,), (0,)), ((), ()))
NN = (((1,), (0,)), ((), ()))


def dot(a, b, dims):
    return lax.dot_general(a, b, dims, preferred_element_type=F32)


def split_dot(a, state, dims):
    high = state.astype(BF16)
    low = (state - high.astype(F32)).astype(BF16)
    return dot(a, high, dims) + dot(a, low, dims)


def causal_mask(rows):
    t = lax.broadcasted_iota(jnp.int32, (rows, rows), 0)
    s = lax.broadcasted_iota(jnp.int32, (rows, rows), 1)
    return s <= t


def head_columns(ref):
    return [ref.at[:, h * DH : (h + 1) * DH] for h in range(ref.shape[1] // DH)]


def outer_kernel(a_ref, b_ref, out_ref):
    for h, (a, b) in enumerate(zip(head_columns(a_ref), head_columns(b_ref))):
        out_ref[h] = dot(a[...], b[...], TN)


def forward_kernel(q_ref, k_ref, v_ref, scale_ref, scaled_ref, intra_ref):
    scaled_ref[...] = (q_ref[...].astype(F32) * scale_ref[...]).astype(BF16)
    mask = causal_mask(scaled_ref.shape[0])
    refs = (scaled_ref, k_ref, v_ref, intra_ref)
    for scaled, keys, values, intra in zip(*map(head_columns, refs)):
        scores = jnp.where(mask, dot(scaled[...], keys[...], NT), 0.0).astype(BF16)
        intra[...] = dot(scores, values[...], NN)


def attended_kernel(scaled_ref, intra_ref, state_ref, out_ref):
    refs = (scaled_ref, intra_ref, out_ref)
    for h, (scaled, intra, out) in enumerate(zip(*map(head_columns, refs))):
        out[...] = (split_dot(scaled[...], state_ref[h], NN) + intra[...]).astype(BF16)


def backward_kernel(
    scaled_ref, k_ref, v_ref, g_ref, scale_ref, state_ref, dq_ref, dk_ref, dv_ref
):
    mask = causal_mask(scaled_ref.shape[0])
    refs = (scaled_ref, k_ref, v_ref, g_ref, dq_ref, dk_ref, dv_ref)
    for h, (scaled, keys, values, grads, dq, dk, dv) in enumerate(zip(*map(head_columns, refs))):
        mixed = jnp.where(mask, dot(grads[...], values[...], NT), 0.0).astype(BF16)
        total = split_dot(grads[...], state_ref[h], NT) + dot(mixed, keys[...], NN)
        dq[...] = (total * scale_ref[...]).astype(BF16)
        dk[...] = dot(mixed, scaled[...], TN)
        scores = jnp.where(mask, dot(scaled[...], keys[...], NT), 0.0).astype(BF16)
        dv[...] = dot(scores, grads[...], TN)


def finish_kernel(k_ref, v_ref, dk_part_ref, dv_part_ref, after_ref, dk_ref, dv_ref):
    refs = (k_ref, v_ref, dk_part_ref, dv_part_ref, dk_ref, dv_ref)
    for h, (keys, values, dk_part, dv_part, dk, dv) in enumerate(zip(*map(head_columns, refs))):
        dk[...] = (split_dot(values[...], after_ref[h], NT) + dk_part[...]).astype(BF16)
        dv[...] = (split_dot(keys[...], after_ref[h], NN) + dv_part[...]).astype(BF16)


def per_head(kernel, rows, heads, ins, outs, macs, step=2):
    if heads % step:
        step = 1
    specs = {
        "h": pl.BlockSpec((rows, step * DH), lambda h: (0, h)),
        "m": pl.BlockSpec((step, DH, DH), lambda h: (h, 0, 0)),
        "s": pl.BlockSpec((rows, 1), lambda h: (0, 0)),
    }
    shapes = {"h": (rows, heads * DH), "m": (heads, DH, DH)}
    return pl.pallas_call(
        kernel,
        grid=(heads // step,),
        in_specs=[specs[kind] for kind in ins],
        out_specs=[specs[kind] for kind, unused in outs],
        out_shape=[jax.ShapeDtypeStruct(shapes[kind], dtype) for kind, dtype in outs],
        compiler_params=pltpu.CompilerParams(vmem_limit_bytes=VMEM_LIMIT),
        cost_estimate=pl.CostEstimate(
            flops=2 * macs * heads,
            bytes_accessed=rows * heads * DH * 2 * (len(ins) + len(outs)),
            transcendentals=0,
        ),
    )


def project_kernel(pieces, half, own_ref, other_ref, *refs):
    def fill(a_ref):
        for piece in range(pieces):
            refs[-1][piece] = dot(a_ref[...], refs[piece][...], NT).astype(BF16)

    pl.when(pl.program_id(0) < half)(lambda: fill(own_ref))
    pl.when(pl.program_id(0) >= half)(lambda: fill(other_ref))


def project(own, other, pieces):
    rows, width = own.shape
    features = pieces[0].shape[0]
    step = min(rows, 256)
    half = rows // step
    return pl.pallas_call(
        functools.partial(project_kernel, len(pieces), half),
        grid=(2 * half,),
        in_specs=[
            pl.BlockSpec((step, width), lambda r: (jnp.minimum(r, half - 1), 0)),
            pl.BlockSpec((step, width), lambda r: (jnp.maximum(r - half, 0), 0)),
        ]
        + [pl.BlockSpec((features, width), lambda r: (0, 0)) for unused in pieces],
        out_specs=pl.BlockSpec((len(pieces), step, features), lambda r: (0, r, 0)),
        out_shape=jax.ShapeDtypeStruct((len(pieces), 2 * rows, features), BF16),
        compiler_params=pltpu.CompilerParams(vmem_limit_bytes=VMEM_LIMIT),
        cost_estimate=pl.CostEstimate(
            flops=4 * rows * width * features * len(pieces),
            bytes_accessed=8 * rows * width,
            transcendentals=0,
        ),
    )(own, other, *pieces)


def products_kernel(count, chips, share, before, factor, meta_ref, *refs):
    candidates, (own_ref, other_ref), rest = refs[:count], refs[count : count + 2], refs[count + 2 :]
    pieces, rest = rest[:chips], rest[chips:]
    earlier, (first_ref, second_ref, grad_ref, total, weight_ref) = rest[:before], rest[before:]
    rows = own_ref.shape[0]
    part = weight_ref.shape[1]
    for delta, piece in enumerate(pieces):
        weight_ref[delta] = piece[...]
    if before:
        total[:rows] = earlier[0][...]
        total[rows:] = earlier[1][...]
    for j, candidate in enumerate(candidates):

        @pl.when(meta_ref[j * (share + 1)] == 1)
        def unused(j=j, candidate=candidate):
            for u in range(share):
                delta = meta_ref[j * (share + 1) + 1 + u]
                values = candidate[:, u * part : (u + 1) * part]
                product = dot(values, weight_ref[delta], NN)
                if j == 0 and u == 0 and not before:
                    total[...] = product
                else:
                    total[...] += product
                grad = dot(values[:rows], own_ref[...], TN) + dot(values[rows:], other_ref[...], TN)
                grad_ref[delta] = (grad * factor).astype(BF16)

    first_ref[...] = total[:rows]
    second_ref[...] = total[rows:].astype(second_ref.dtype)


def products(meta, candidates, own, other, weights, earlier, second_type, factor, share):
    rows, width = own.shape
    chips, part = len(weights), weights[0].shape[0]
    step = 256 if width % 256 == 0 else DH
    block = pl.BlockSpec((rows, step), lambda k, unused: (0, k))
    pieces = pl.BlockSpec((chips, part, step), lambda k, unused: (0, 0, k))
    return pl.pallas_call(
        functools.partial(products_kernel, len(candidates), chips, share, len(earlier), factor),
        grid_spec=pltpu.PrefetchScalarGridSpec(
            num_scalar_prefetch=1,
            grid=(width // step,),
            in_specs=[pl.BlockSpec(c.shape, lambda k, unused: (0, 0)) for c in candidates]
            + [block, block]
            + [pl.BlockSpec((part, step), lambda k, unused: (0, k)) for unused in weights]
            + [block for unused in earlier],
            out_specs=[block, block, pieces],
            scratch_shapes=[pltpu.VMEM((2 * rows, step), F32), pltpu.VMEM((chips, part, step), BF16)],
        ),
        out_shape=[
            jax.ShapeDtypeStruct((rows, width), F32),
            jax.ShapeDtypeStruct((rows, width), second_type),
            jax.ShapeDtypeStruct((chips, part, width), BF16),
        ],
        compiler_params=pltpu.CompilerParams(vmem_limit_bytes=2 * VMEM_LIMIT),
        cost_estimate=pl.CostEstimate(
            flops=8 * rows * width * part * chips,
            bytes_accessed=16 * rows * width,
            transcendentals=0,
        ),
    )(meta, *candidates, own, other, *weights, *earlier)


def core_swap(value):
    count = lax.axis_size("seq")
    return lax.ppermute(value, "seq", [(j, j ^ 1) for j in range(count)])


def chip_swap(value, delta):
    count = lax.axis_size("seq")
    return lax.ppermute(value, "seq", [(j, j ^ (2 * delta)) for j in range(count)])


def line_permutes(active):
    even = [pair for pair in active if min(pair) % 2 == 0]
    odd = [pair for pair in active if min(pair) % 2 == 1]
    return even, odd


def line_step(values, active):
    return [
        lax.ppermute(value, "head", pairs) if pairs else None
        for value, pairs in zip(values, line_permutes(active))
    ]


def line_sum(part_for, beside):
    count = lax.axis_size("head")
    mine = lax.axis_index("head")
    got = [None, None]
    for step in range(1, count):
        active = [(j, j + 1) for j in range(count - 1) if j <= step - 1]
        active += [(j, j - 1) for j in range(1, count) if count - 1 - j <= step - 1]
        values = []
        for parity, pairs in enumerate(line_permutes(active)):
            if not pairs:
                values.append(None)
                continue
            target = jnp.where(mine % 2 == parity, mine + count - step, mine - count + step)
            value = part_for(jnp.clip(target, 0, count - 1))
            if got[1 - parity] is not None:
                value = (value.astype(F32) + got[1 - parity].astype(F32)).astype(BF16)
            values.append(value)
        got = line_step(values, active)
        if beside.get(step):
            got, unused = lax.optimization_barrier((got, beside[step]))
    total = part_for(mine).astype(F32)
    for value in got:
        if value is not None:
            total = total + value.astype(F32)
    return total


def line_gather(value, tied):
    tied = dict(tied)
    count = lax.axis_size("head")
    mine = lax.axis_index("head")
    found, arrived = [(value, mine >= 0, mine)], {}
    got = [value, value]
    for step in range(1, count):
        active = [(j, j + 1) for j in range(count - 1) if j >= step - 1]
        active += [(j, j - 1) for j in range(1, count) if j + step - 1 <= count - 1]
        new = line_step([value if got[1 - q] is None else got[1 - q] for q in (0, 1)], active)
        if step in tied:
            new, tied[step] = lax.optimization_barrier((new, tied[step]))
        got = new
        arrived[step] = [item for item in got if item is not None]
        for parity, item in enumerate(got):
            if item is None:
                continue
            source = jnp.where(mine % 2 == parity, mine + step, mine - step)
            found.append((item, (source >= 0) & (source < count), source))
    return found, arrived, tied


def swapped_halves(total):
    core = lax.rem(lax.axis_index("seq"), 2)
    half_heads = total.shape[0] // 2
    mine = total.astype(BF16)
    other = core_swap(mine)
    both = mine.astype(F32) + other.astype(F32)
    half = lax.dynamic_slice_in_dim(both, core * half_heads, half_heads, 0).astype(BF16)
    return half, other


def sum_of_others(half, arrived, other, lower):
    position = lax.axis_index("seq")
    chip, core = lax.div(position, 2), lax.rem(position, 2)
    summed = jnp.zeros(half.shape, F32)
    for delta, item in enumerate(arrived, 1):
        partner = chip ^ delta
        counts = (partner < chip) if lower else (partner > chip)
        summed = summed + jnp.where(counts, item.astype(F32), 0.0)
    summed = summed.astype(BF16)
    swapped = core_swap(summed)
    first = jnp.where(core == 0, summed, swapped)
    second = jnp.where(core == 0, swapped, summed)
    whole = jnp.concatenate([first, second], axis=0).astype(F32)
    return whole + jnp.where(core == (1 if lower else 0), other.astype(F32), 0.0)


def near_pieces(own):
    chips = lax.axis_size("seq") // 2
    if chips != 4:
        pieces = [own] + [chip_swap(own, delta) for delta in range(1, chips)]
        return pieces[1:], lambda arrived: [own, *arrived]
    half = own.shape[0] // 2

    def rest(arrived):
        first = chip_swap(arrived[0][:half], 2)
        second = chip_swap(arrived[1][half:], 1)
        return [own, *arrived, jnp.concatenate([first, second], axis=0)]

    return [chip_swap(own, 1), chip_swap(own, 2)], rest


def scatter_start(grads):
    chips, part = grads.shape[:2]
    if chips != 4:
        sent = [chip_swap(grads[delta], delta) for delta in range(1, chips)]
        return sent, lambda arrived: (arrived, lambda final: added(grads[0], *final))
    half = part // 2
    upper, lower = slice(0, half), slice(half, part)
    sent = [chip_swap(grads[1::2, upper], 1), chip_swap(grads[2:, lower], 2)]

    def second(arrived):
        by_x, by_y = arrived
        upper_sum = added(grads[2, upper], by_x[1]).astype(BF16)
        lower_sum = added(grads[1, lower], by_y[1]).astype(BF16)

        def finish(final):
            return jnp.concatenate(
                [
                    added(grads[0, upper], by_x[0], final[0]),
                    added(grads[0, lower], by_y[0], final[1]),
                ],
                axis=0,
            )

        return [chip_swap(upper_sum, 2), chip_swap(lower_sum, 1)], finish

    return sent, second


def added(*values):
    return sum(value.astype(F32) for value in values)


def on_device(query_rows, key_rows, value_rows, out_weight, target_rows):
    rows, width = query_rows.shape
    heads = width // DH
    groups = lax.axis_size("head")
    seq_count = lax.axis_size("seq")
    chips = seq_count // 2
    share = chips // groups
    position = lax.axis_index("seq")
    chip, core = lax.div(position, 2), lax.rem(position, 2)
    held = out_weight.shape[0]
    part = held // CHUNKS
    call = functools.partial(per_head, rows=rows, heads=heads)
    barrier = lax.optimization_barrier
    outer = call(outer_kernel, ins="hh", outs=[("m", F32)], macs=rows * DH * DH, step=4)

    positions = (position * rows + jnp.arange(rows, dtype=jnp.int32) + 1).astype(F32)
    scale = lax.rsqrt(F32(DH) * positions)[:, None]
    (key_value,) = outer(key_rows, value_rows)
    half, other = swapped_halves(key_value)
    arrived = [chip_swap(half, delta) for delta in range(1, chips)]
    near, rest = near_pieces(out_weight[:part])
    scaled, intra = call(
        forward_kernel, ins="hhhs", outs=[("h", BF16), ("h", F32)], macs=2 * rows * rows * DH
    )(query_rows, key_rows, value_rows, scale)
    arrived, near, scaled, intra = barrier((arrived, near, scaled, intra))
    pieces = rest(near)
    before = sum_of_others(half, arrived, other, True)
    (attended,) = call(
        attended_kernel, ins="hhm", outs=[("h", BF16)], macs=2 * rows * DH * DH, step=4
    )(scaled, intra, before)
    other_attended = core_swap(attended)

    targets = target_rows.reshape(rows, share, 2, held)
    own_target = lax.dynamic_index_in_dim(targets, core, 2, keepdims=False)
    sent_target = lax.dynamic_index_in_dim(targets, 1 - core, 2, keepdims=False)
    both_targets = jnp.concatenate([own_target, core_swap(sent_target)], axis=0)

    outputs, grad_parts = [], []
    gate, totals, sent, gathered = None, (), None, {}
    factor = 1.0 / math.sqrt(rows * seq_count)
    for c in range(CHUNKS):
        last = c == CHUNKS - 1
        if c:
            own_rows, unused = barrier((out_weight[c * part : (c + 1) * part], pieces[-1]))
            near, rest = near_pieces(own_rows)
            pieces = rest(near)
        partial_out = project(attended, other_attended, pieces)
        if gate is not None:
            partial_out, gate, outputs[-1] = barrier((partial_out, gate, outputs[-1]))

        def part_for(group, partial_out=partial_out):
            found = [
                lax.dynamic_index_in_dim(partial_out, (group * share + j) ^ chip, 0, keepdims=False)
                for j in range(share)
            ]
            return found[0] if share == 1 else jnp.concatenate(found, axis=1)

        summed = line_sum(part_for, {step - 1: items for step, items in gathered.items() if step > 1}).astype(BF16)
        target = both_targets[:, :, c * part : (c + 1) * part].reshape(2 * rows, share * part)
        residual = (summed.astype(F32) - target.astype(F32)).astype(BF16)
        own_output = summed[:rows].reshape(rows, share, part)
        other_output = core_swap(summed[rows:]).reshape(rows, share, part)
        first = jnp.where(core == 0, own_output, other_output)
        second = jnp.where(core == 0, other_output, own_output)
        outputs.append(jnp.stack([first, second], axis=2))
        output = jnp.concatenate(outputs, axis=3).reshape(rows, width) if last else None
        found, gathered, tied = line_gather(
            residual, {1: totals, 2: (sent, output)}
        )
        totals, (sent, output) = tied[1], tied[2]
        gate = gathered[1]
        meta = []
        for unused, valid, source in found:
            meta.append(valid.astype(jnp.int32))
            meta += [
                jnp.clip((source * share + j) ^ chip, 0, chips - 1).astype(jnp.int32)
                for j in range(share)
            ]
        items = [item for item, unused, unused in found]
        if sent is not None:
            sent, finish = second_step(sent)
            items, sent = barrier((items, sent))
            grad_parts.append(finish(sent))
        *totals, grads = products(
            jnp.stack(meta),
            items,
            attended,
            other_attended,
            pieces,
            totals,
            BF16 if last else F32,
            factor,
            share,
        )
        sent, second_step = scatter_start(grads)

    grad_attended = (totals[0] + core_swap(totals[1]).astype(F32)).astype(BF16)
    (query_grad,) = outer(scaled, grad_attended)
    half, other = swapped_halves(query_grad)
    arrived = [chip_swap(half, delta) for delta in range(1, chips)]
    grad_query, key_part, value_part = call(
        backward_kernel,
        ins="hhhhsm",
        outs=[("h", BF16), ("h", F32), ("h", F32)],
        macs=5 * rows * rows * DH,
    )(scaled, key_rows, value_rows, grad_attended, scale, before)
    arrived, key_part, value_part, grad_query, sent = barrier(
        (arrived, key_part, value_part, grad_query, sent)
    )
    sent, finish = second_step(sent)
    after = sum_of_others(half, arrived, other, False)
    sent, after = barrier((sent, after))
    grad_key, grad_value = call(
        finish_kernel, ins="hhhhm", outs=[("h", BF16), ("h", BF16)], macs=4 * rows * DH * DH
    )(key_rows, value_rows, key_part, value_part, after)
    grad_weight = jnp.concatenate([*grad_parts, finish(sent)], axis=0)
    return output, grad_query, grad_key, grad_value, grad_weight


def solution(mesh):
    placed = P("seq", "head")
    return jax.shard_map(
        on_device,
        mesh=mesh,
        in_specs=(placed,) * 5,
        out_specs=(placed,) * 5,
        check_vma=False,
    )
```

```python
import functools
import math

import jax
import jax.numpy as jnp
from jax import lax
from jax.experimental import pallas as pl
from jax.experimental.pallas import tpu as pltpu
from jax.sharding import PartitionSpec as P

DH = 128
CHUNKS = 2
F32 = jnp.float32
BF16 = jnp.bfloat16
VMEM_LIMIT = 16 * 1024 * 1024

NT = (((1,), (1,)), ((), ()))
TN = (((0,), (0,)), ((), ()))
NN = (((1,), (0,)), ((), ()))


def in_hbm(values):
    return [pltpu.with_memory_space_constraint(value, pltpu.HBM) for value in values]


def dot(a, b, dims):
    return lax.dot_general(a, b, dims, preferred_element_type=F32)


def split_dot(a, state, dims):
    high = state.astype(BF16)
    low = (state - high.astype(F32)).astype(BF16)
    return dot(a, high, dims) + dot(a, low, dims)


def head_columns(ref):
    return [ref.at[:, h * DH : (h + 1) * DH] for h in range(ref.shape[1] // DH)]


def outer_kernel(a_ref, b_ref, out_ref):
    for h, (a, b) in enumerate(zip(head_columns(a_ref), head_columns(b_ref))):
        out_ref[h] = dot(a[...], b[...], TN)


def halves(rows):
    middle = rows // 2
    return [(slice(0, middle), slice(0, middle)), (slice(middle, rows), slice(0, rows))]


def masked(product):
    rows, columns = product.shape
    t = lax.broadcasted_iota(jnp.int32, product.shape, 0) + (columns - rows)
    s = lax.broadcasted_iota(jnp.int32, product.shape, 1)
    return jnp.where(s <= t, product, 0.0).astype(BF16)


def forward_kernel(q_ref, k_ref, v_ref, scale_ref, scaled_ref, intra_ref):
    scaled_ref[...] = (q_ref[...].astype(F32) * scale_ref[...]).astype(BF16)
    refs = (scaled_ref, k_ref, v_ref, intra_ref)
    for scaled, keys, values, intra in zip(*map(head_columns, refs)):
        for own, upto in halves(scaled_ref.shape[0]):
            scores = masked(dot(scaled[own], keys[upto], NT))
            intra[own] = dot(scores, values[upto], NN)


def attended_kernel(scaled_ref, intra_ref, state_ref, out_ref):
    refs = (scaled_ref, intra_ref, out_ref)
    for h, (scaled, intra, out) in enumerate(zip(*map(head_columns, refs))):
        out[...] = (split_dot(scaled[...], state_ref[h], NN) + intra[...]).astype(BF16)


def backward_kernel(
    scaled_ref, k_ref, v_ref, g_ref, scale_ref, state_ref, dq_ref, dk_ref, dv_ref
):
    rows = scaled_ref.shape[0]
    refs = (scaled_ref, k_ref, v_ref, g_ref, dq_ref, dk_ref, dv_ref)
    for h, (scaled, keys, values, grads, dq, dk, dv) in enumerate(zip(*map(head_columns, refs))):
        inter = split_dot(grads[...], state_ref[h], NT)
        for own, upto in reversed(halves(rows)):
            mixed = masked(dot(grads[own], values[upto], NT))
            scores = masked(dot(scaled[own], keys[upto], NT))
            total = inter[own] + dot(mixed, keys[upto], NN)
            dq[own] = (total * scale_ref[own]).astype(BF16)
            key_part = dot(mixed, scaled[own], TN)
            value_part = dot(scores, grads[own], TN)
            if upto.stop == rows:
                dk[...] = key_part
                dv[...] = value_part
            else:
                dk[upto] += key_part
                dv[upto] += value_part


def finish_kernel(k_ref, v_ref, dk_part_ref, dv_part_ref, after_ref, dk_ref, dv_ref):
    refs = (k_ref, v_ref, dk_part_ref, dv_part_ref, dk_ref, dv_ref)
    for h, (keys, values, dk_part, dv_part, dk, dv) in enumerate(zip(*map(head_columns, refs))):
        dk[...] = (split_dot(values[...], after_ref[h], NT) + dk_part[...]).astype(BF16)
        dv[...] = (split_dot(keys[...], after_ref[h], NN) + dv_part[...]).astype(BF16)


def per_head(kernel, rows, heads, ins, outs, macs, step=2):
    if heads % step:
        step = 1
    specs = {
        "h": pl.BlockSpec((rows, step * DH), lambda h: (0, h)),
        "m": pl.BlockSpec((step, DH, DH), lambda h: (h, 0, 0)),
        "s": pl.BlockSpec((rows, 1), lambda h: (0, 0)),
    }
    shapes = {"h": (rows, heads * DH), "m": (heads, DH, DH)}
    call = pl.pallas_call(
        kernel,
        grid=(heads // step,),
        in_specs=[specs[kind] for kind in ins],
        out_specs=[specs[kind] for kind, unused in outs],
        out_shape=[
            (pltpu.HBM if kind == "h" else jax.ShapeDtypeStruct)(shapes[kind], dtype)
            for kind, dtype in outs
        ],
        compiler_params=pltpu.CompilerParams(vmem_limit_bytes=VMEM_LIMIT),
        cost_estimate=pl.CostEstimate(
            flops=2 * macs * heads,
            bytes_accessed=rows * heads * DH * 2 * (len(ins) + len(outs)),
            transcendentals=0,
        ),
    )

    def on_values(*values):
        return call(
            *[in_hbm([value])[0] if kind == "h" else value for kind, value in zip(ins, values)]
        )

    return on_values


def project_kernel(pieces, half, own_ref, other_ref, *refs):
    def fill(a_ref):
        for piece in range(pieces):
            refs[-1][piece] = dot(a_ref[...], refs[piece][...], NT).astype(BF16)

    pl.when(pl.program_id(0) < half)(lambda: fill(own_ref))
    pl.when(pl.program_id(0) >= half)(lambda: fill(other_ref))


def project(own, other, pieces):
    rows, width = own.shape
    features = pieces[0].shape[0]
    step = min(rows, 256)
    half = rows // step
    return pl.pallas_call(
        functools.partial(project_kernel, len(pieces), half),
        grid=(2 * half,),
        in_specs=[
            pl.BlockSpec((step, width), lambda r: (jnp.minimum(r, half - 1), 0)),
            pl.BlockSpec((step, width), lambda r: (jnp.maximum(r - half, 0), 0)),
        ]
        + [pl.BlockSpec((features, width), lambda r: (0, 0)) for unused in pieces],
        out_specs=pl.BlockSpec((len(pieces), step, features), lambda r: (0, r, 0)),
        out_shape=jax.ShapeDtypeStruct((len(pieces), 2 * rows, features), BF16),
        compiler_params=pltpu.CompilerParams(vmem_limit_bytes=VMEM_LIMIT),
        cost_estimate=pl.CostEstimate(
            flops=4 * rows * width * features * len(pieces),
            bytes_accessed=8 * rows * width,
            transcendentals=0,
        ),
    )(*in_hbm([own, other, *pieces]))


def products_kernel(count, late, chips, before, factor, meta_ref, *refs):
    candidates, (own_ref, other_ref), rest = refs[:count], refs[count : count + 2], refs[count + 2 :]
    weights, rest = rest[:chips], rest[chips:]
    earlier, rest = rest[:before], rest[before:]
    first_ref, second_ref, grad_ref, gathered, turned, semaphores = rest
    rows = own_ref.shape[0]
    part = weights[0].shape[0]

    @pl.when(pl.program_id(0) == 0)
    def unused():
        copies = []
        for j, candidate in enumerate(candidates):
            for u in range(candidate.shape[1] // part):
                copies.append(
                    (
                        meta_ref[2 * len(copies)] == 1,
                        pltpu.make_async_copy(
                            candidate.at[:, u * part : (u + 1) * part],
                            gathered.at[meta_ref[2 * len(copies) + 1]],
                            semaphores.at[len(copies)],
                        ),
                    )
                )
        for valid, copy in copies:
            pl.when(valid)(copy.start)
        for j in range(len(copies), len(copies) + late):

            @pl.when(meta_ref[2 * j] == 1)
            def unused_zero(j=j):
                gathered[meta_ref[2 * j + 1]] = jnp.zeros(gathered.shape[1:], BF16)

        for valid, copy in copies:
            pl.when(valid)(copy.wait)
        for delta in range(chips):
            turned[delta * part : (delta + 1) * part, :] = gathered[delta].T

    residuals = jnp.concatenate([gathered[delta] for delta in range(chips)], axis=1)
    weight = jnp.concatenate([piece[...] for piece in weights], axis=0)
    total = dot(residuals, weight, NN)
    first, second = total[:rows], total[rows:]
    if before:
        first, second = first + earlier[0][...], second + earlier[1][...]
    first_ref[...] = first
    second_ref[...] = second
    grad = dot(turned[:, :rows], own_ref[...], NN) + dot(turned[:, rows:], other_ref[...], NN)
    grad = (grad * factor).astype(BF16)
    for delta in range(chips):
        grad_ref[delta] = grad[delta * part : (delta + 1) * part]


def products(meta, candidates, late, own, other, weights, earlier, factor):
    rows, width = own.shape
    chips, part = len(weights), weights[0].shape[0]
    step = 256 if width % 256 == 0 else DH
    block = pl.BlockSpec((rows, step), lambda k, unused: (0, k))
    pieces = pl.BlockSpec((chips, part, step), lambda k, unused: (0, 0, k))
    copies = sum(c.shape[1] for c in candidates) // part
    return pl.pallas_call(
        functools.partial(products_kernel, len(candidates), late, chips, len(earlier), factor),
        grid_spec=pltpu.PrefetchScalarGridSpec(
            num_scalar_prefetch=1,
            grid=(width // step,),
            in_specs=[pl.BlockSpec(memory_space=pltpu.HBM) for unused in candidates]
            + [block, block]
            + [pl.BlockSpec((part, step), lambda k, unused: (0, k)) for unused in weights]
            + [block for unused in earlier],
            out_specs=[block, block, pieces],
            scratch_shapes=[
                pltpu.VMEM((chips, 2 * rows, part), BF16),
                pltpu.VMEM((chips * part, 2 * rows), BF16),
                pltpu.SemaphoreType.DMA((copies,)),
            ],
        ),
        out_shape=[
            pltpu.HBM((rows, width), F32),
            pltpu.HBM((rows, width), F32),
            pltpu.HBM((chips, part, width), BF16),
        ],
        compiler_params=pltpu.CompilerParams(vmem_limit_bytes=32 * rows * chips * part),
        cost_estimate=pl.CostEstimate(
            flops=8 * rows * width * part * chips,
            bytes_accessed=16 * rows * width,
            transcendentals=0,
        ),
    )(meta, *in_hbm([*candidates, own, other, *weights, *earlier]))


def late_kernel(
    chips, factor, second_type, meta_ref, piece_ref, own_ref, other_ref, first_in, second_in, grad_in, *refs
):
    weights, (first_ref, second_ref, grad_ref) = refs[:chips], refs[chips:]
    rows = own_ref.shape[0]
    valid, place = meta_ref[0] == 1, meta_ref[1]

    @pl.when(jnp.logical_not(valid))
    def unused_pass():
        first_ref[...] = first_in[...]
        second_ref[...] = second_in[...].astype(second_type)
        grad_ref[...] = grad_in[...]

    for delta, weight in enumerate(weights):

        @pl.when(valid & (place == delta))
        def unused_add(weight=weight):
            total = dot(piece_ref[...], weight[...], NN)
            first_ref[...] = first_in[...] + total[:rows]
            second_ref[...] = (second_in[...] + total[rows:]).astype(second_type)

    @pl.when(valid)
    def unused_grad():
        grad = dot(piece_ref[:rows], own_ref[...], TN) + dot(piece_ref[rows:], other_ref[...], TN)
        grad_ref[0] = (grad * factor).astype(BF16)


def late_products(meta, piece, own, other, weights, totals, grads, second_type, factor):
    rows, width = own.shape
    chips, part = len(weights), weights[0].shape[0]
    step = min(width, 512)
    block = pl.BlockSpec((rows, step), lambda k, unused: (0, k))
    slot = pl.BlockSpec((1, part, step), lambda k, meta: (meta[1], 0, k))
    return pl.pallas_call(
        functools.partial(late_kernel, chips, factor, second_type),
        grid_spec=pltpu.PrefetchScalarGridSpec(
            num_scalar_prefetch=1,
            grid=(width // step,),
            in_specs=[pl.BlockSpec(piece.shape, lambda k, unused: (0, 0)), block, block, block, block, slot]
            + [pl.BlockSpec((part, step), lambda k, unused: (0, k)) for unused in weights],
            out_specs=[block, block, slot],
        ),
        out_shape=[
            pltpu.HBM((rows, width), F32),
            pltpu.HBM((rows, width), second_type),
            pltpu.HBM(grads.shape, BF16),
        ],
        input_output_aliases={6: 2},
        compiler_params=pltpu.CompilerParams(vmem_limit_bytes=VMEM_LIMIT),
        cost_estimate=pl.CostEstimate(
            flops=8 * rows * width * part,
            bytes_accessed=16 * rows * width,
            transcendentals=0,
        ),
    )(meta, piece, *in_hbm([own, other, *totals, grads, *weights]))


def core_swap(value):
    count = lax.axis_size("seq")
    return lax.ppermute(value, "seq", [(j, j ^ 1) for j in range(count)])


def chip_swap(value, delta):
    count = lax.axis_size("seq")
    return lax.ppermute(value, "seq", [(j, j ^ (2 * delta)) for j in range(count)])


def line_permutes(active):
    even = [pair for pair in active if min(pair) % 2 == 0]
    odd = [pair for pair in active if min(pair) % 2 == 1]
    return even, odd


def line_step(values, active):
    return [
        lax.ppermute(value, "head", pairs) if pairs else None
        for value, pairs in zip(values, line_permutes(active))
    ]


def line_sum(part_for, beside):
    count = lax.axis_size("head")
    mine = lax.axis_index("head")
    got = [None, None]
    for step in range(1, count):
        active = [(j, j + 1) for j in range(count - 1) if j <= step - 1]
        active += [(j, j - 1) for j in range(1, count) if count - 1 - j <= step - 1]
        values = []
        for parity, pairs in enumerate(line_permutes(active)):
            if not pairs:
                values.append(None)
                continue
            target = jnp.where(mine % 2 == parity, mine + count - step, mine - count + step)
            value = part_for(jnp.clip(target, 0, count - 1))
            if step > 1 and got[1 - parity] is None:
                value, unused = lax.optimization_barrier((value, got[parity]))
            elif step > 1:
                value = (value.astype(F32) + got[1 - parity].astype(F32)).astype(BF16)
            values.append(value)
        got = line_step(values, active)
        if beside.get(step):
            got, unused = lax.optimization_barrier((got, beside[step]))
    total = part_for(mine).astype(F32)
    for value in got:
        if value is not None:
            total = total + value.astype(F32)
    return total


def line_gather(value, tied):
    tied = dict(tied)
    count = lax.axis_size("head")
    mine = lax.axis_index("head")
    found, arrived = [(value, mine >= 0, mine)], {}
    got = [value, value]
    for step in range(1, count):
        active = [(j, j + 1) for j in range(count - 1) if j >= step - 1]
        active += [(j, j - 1) for j in range(1, count) if j + step - 1 <= count - 1]
        new = line_step([value if got[1 - q] is None else got[1 - q] for q in (0, 1)], active)
        if step in tied:
            new, tied[step] = lax.optimization_barrier((new, tied[step]))
        got = new
        arrived[step] = [item for item in got if item is not None]
        for parity, item in enumerate(got):
            if item is None:
                continue
            source = jnp.where(mine % 2 == parity, mine + step, mine - step)
            found.append((item, (source >= 0) & (source < count), source))
    return found, arrived, tied


def swapped_halves(total):
    core = lax.rem(lax.axis_index("seq"), 2)
    half_heads = total.shape[0] // 2
    mine = total.astype(BF16)
    other = core_swap(mine)
    both = mine.astype(F32) + other.astype(F32)
    half = lax.dynamic_slice_in_dim(both, core * half_heads, half_heads, 0).astype(BF16)
    return half, other


def sum_of_others(half, arrived, other, lower):
    position = lax.axis_index("seq")
    chip, core = lax.div(position, 2), lax.rem(position, 2)
    summed = jnp.zeros(half.shape, F32)
    for delta, item in enumerate(arrived, 1):
        partner = chip ^ delta
        counts = (partner < chip) if lower else (partner > chip)
        summed = summed + jnp.where(counts, item.astype(F32), 0.0)
    summed = summed.astype(BF16)
    swapped = core_swap(summed)
    first = jnp.where(core == 0, summed, swapped)
    second = jnp.where(core == 0, swapped, summed)
    whole = jnp.concatenate([first, second], axis=0).astype(F32)
    return whole + jnp.where(core == (1 if lower else 0), other.astype(F32), 0.0)


def near_pieces(own):
    chips = lax.axis_size("seq") // 2
    if chips != 4:
        pieces = [own] + [chip_swap(own, delta) for delta in range(1, chips)]
        return pieces[1:], lambda arrived: [own, *arrived]
    half = own.shape[0] // 2

    def rest(arrived):
        first = chip_swap(arrived[0][:half], 2)
        second = chip_swap(arrived[1][half:], 1)
        return [own, *arrived, jnp.concatenate([first, second], axis=0)]

    return [chip_swap(own, 1), chip_swap(own, 2)], rest


def scatter_start(grads):
    chips, part = grads.shape[:2]
    if chips != 4:
        sent = [chip_swap(grads[delta], delta) for delta in range(1, chips)]
        return sent, lambda arrived: (arrived, lambda final: added(grads[0], *final))
    half = part // 2
    upper, lower = slice(0, half), slice(half, part)
    sent = [chip_swap(grads[1::2, upper], 1), chip_swap(grads[2:, lower], 2)]

    def second(arrived):
        by_x, by_y = arrived
        upper_sum = added(grads[2, upper], by_x[1]).astype(BF16)
        lower_sum = added(grads[1, lower], by_y[1]).astype(BF16)

        def finish(final):
            return jnp.concatenate(
                [
                    added(grads[0, upper], by_x[0], final[0]),
                    added(grads[0, lower], by_y[0], final[1]),
                ],
                axis=0,
            )

        return [chip_swap(upper_sum, 2), chip_swap(lower_sum, 1)], finish

    return sent, second


def added(*values):
    return sum(value.astype(F32) for value in values)


def on_device(query_rows, key_rows, value_rows, out_weight, target_rows):
    rows, width = query_rows.shape
    heads = width // DH
    groups = lax.axis_size("head")
    seq_count = lax.axis_size("seq")
    chips = seq_count // 2
    share = chips // groups
    position = lax.axis_index("seq")
    chip, core = lax.div(position, 2), lax.rem(position, 2)
    held = out_weight.shape[0]
    chunks = CHUNKS if held % (CHUNKS * DH) == 0 else 1
    part = held // chunks
    call = functools.partial(per_head, rows=rows, heads=heads)
    barrier = lax.optimization_barrier
    outer = call(outer_kernel, ins="hh", outs=[("m", F32)], macs=rows * DH * DH, step=4)

    positions = (position * rows + jnp.arange(rows, dtype=jnp.int32) + 1).astype(F32)
    scale = lax.rsqrt(F32(DH) * positions)[:, None]
    (key_value,) = outer(key_rows, value_rows)
    half, other = swapped_halves(key_value)
    arrived = [chip_swap(half, delta) for delta in range(1, chips)]
    near, rest = near_pieces(out_weight[:part])
    scaled, intra = call(
        forward_kernel, ins="hhhs", outs=[("h", BF16), ("h", F32)], macs=2 * rows * rows * DH
    )(query_rows, key_rows, value_rows, scale)
    def features_of(array, group, first, count):
        found = [
            lax.dynamic_slice_in_dim(array, (2 * j + group) * held + first, count, 1)
            for j in range(share)
        ]
        return found[0] if share == 1 else jnp.concatenate(found, axis=1)

    def chunk_of(array, c):
        found = [array[:, j * held + c * part : j * held + (c + 1) * part] for j in range(share)]
        return found[0] if share == 1 else jnp.concatenate(found, axis=1)

    other_targets = core_swap(features_of(target_rows, 1 - core, 0, held))
    targets = [
        jnp.concatenate(
            [features_of(target_rows, core, c * part, part), chunk_of(other_targets, c)], axis=0
        )
        for c in range(chunks)
    ]
    near, scaled, intra = barrier((near, scaled, intra))
    pieces = rest(near)
    arrived, targets, scaled = barrier((arrived, targets, scaled))
    before = sum_of_others(half, arrived, other, True)
    before, pieces = barrier((before, pieces))
    (attended,) = call(
        attended_kernel, ins="hhm", outs=[("h", BF16)], macs=2 * rows * DH * DH, step=4
    )(scaled, intra, before)
    other_attended = core_swap(attended)

    outputs, grad_parts = [], []
    gate, totals, sent, gathered = None, (), None, {}
    factor = 1.0 / math.sqrt(rows * seq_count)
    for c in range(chunks):
        last = c == chunks - 1
        if c:
            own_rows, unused = barrier((out_weight[c * part : (c + 1) * part], pieces[-1]))
            near, rest = near_pieces(own_rows)
            pieces = rest(near)
        partial_out = project(attended, other_attended, pieces)
        if gate is not None:
            partial_out, gate, outputs[-1] = barrier((partial_out, gate, outputs[-1]))

        def part_for(group, partial_out=partial_out):
            found = [
                lax.dynamic_index_in_dim(partial_out, (group * share + j) ^ chip, 0, keepdims=False)
                for j in range(share)
            ]
            return found[0] if share == 1 else jnp.concatenate(found, axis=1)

        summed = line_sum(part_for, {step - 1: items for step, items in gathered.items() if step > 1}).astype(BF16)
        residual = (summed.astype(F32) - targets[c].astype(F32)).astype(BF16)
        own_output = summed[:rows]
        other_output = core_swap(summed[rows:])
        outputs.append(
            [
                jnp.where(core == 0, own_output, other_output),
                jnp.where(core == 0, other_output, own_output),
            ]
        )
        output = None
        if last:
            output = jnp.concatenate(
                [
                    piece[group][:, j * part : (j + 1) * part]
                    for j in range(share)
                    for group in (0, 1)
                    for piece in outputs
                ],
                axis=1,
            )
        found, gathered, tied = line_gather(
            residual, {1: totals, 2: (sent, output)}
        )
        totals, (sent, output) = tied[1], tied[2]
        gate = gathered[1]
        weights = pieces
        on_time = found[:-1] if last and len(found) > 1 else found
        metas = [
            [
                value
                for j in range(share)
                for value in (
                    valid.astype(jnp.int32),
                    jnp.clip((source * share + j) ^ chip, 0, chips - 1).astype(jnp.int32),
                )
            ]
            for unused, valid, source in found
        ]
        late = found[len(on_time) :]
        if not last:
            items = [item for item, unused, unused in on_time]
            if sent is not None:
                sent, finish = second_step(sent)
                items, sent = barrier((items, sent))
                grad_parts.append(finish(sent))
        else:
            items = [item for item, unused, unused in on_time]
        *totals, grads = products(
            jnp.stack(sum(metas, [])),
            items,
            len(late) * share,
            attended,
            other_attended,
            weights,
            totals,
            factor,
        )
        if late:
            item = late[0][0]
            if sent is not None:
                sent, finish = second_step(sent)
                item, sent, totals = barrier((item, sent, totals))
                grad_parts.append(finish(sent))
            for j in range(share):
                *totals, grads = late_products(
                    jnp.stack(metas[-1][2 * j : 2 * j + 2]),
                    item[:, j * part : (j + 1) * part] if share > 1 else item,
                    attended,
                    other_attended,
                    weights,
                    totals,
                    grads,
                    BF16 if j == share - 1 else F32,
                    factor,
                )
        sent, second_step = scatter_start(grads)

    grad_attended = (totals[0] + core_swap(totals[1]).astype(F32)).astype(BF16)
    (query_grad,) = outer(scaled, grad_attended)
    half, other = swapped_halves(query_grad)
    arrived = [chip_swap(half, delta) for delta in range(1, chips)]
    grad_query, key_part, value_part = call(
        backward_kernel,
        ins="hhhhsm",
        outs=[("h", BF16), ("h", F32), ("h", F32)],
        macs=5 * rows * rows * DH,
    )(scaled, key_rows, value_rows, grad_attended, scale, before)
    arrived, key_part, value_part, grad_query, sent = barrier(
        (arrived, key_part, value_part, grad_query, sent)
    )
    sent, finish = second_step(sent)
    after = sum_of_others(half, arrived, other, False)
    grad_key, grad_value = call(
        finish_kernel, ins="hhhhm", outs=[("h", BF16), ("h", BF16)], macs=4 * rows * DH * DH
    )(key_rows, value_rows, key_part, value_part, after)
    sent, grad_key, grad_value = barrier((sent, grad_key, grad_value))
    grad_weight = jnp.concatenate([*grad_parts, finish(sent)], axis=0)
    return output, grad_query, grad_key, grad_value, grad_weight


def solution(mesh):
    placed = P("seq", "head")
    return jax.shard_map(
        on_device,
        mesh=mesh,
        in_specs=(placed,) * 5,
        out_specs=(placed,) * 5,
        check_vma=False,
    )
```

```python
import functools
import math

import jax
import jax.numpy as jnp
from jax import lax
from jax.experimental import pallas as pl
from jax.experimental.pallas import tpu as pltpu
from jax.sharding import PartitionSpec as P

DH = 128
CHUNKS = 2
F32 = jnp.float32
BF16 = jnp.bfloat16
VMEM_LIMIT = 16 * 1024 * 1024

NT = (((1,), (1,)), ((), ()))
TN = (((0,), (0,)), ((), ()))
NN = (((1,), (0,)), ((), ()))


def in_hbm(values):
    return [pltpu.with_memory_space_constraint(value, pltpu.HBM) for value in values]


def dot(a, b, dims):
    return lax.dot_general(a, b, dims, preferred_element_type=F32)


def split_dot(a, state, dims):
    high = state.astype(BF16)
    low = (state - high.astype(F32)).astype(BF16)
    return dot(a, high, dims) + dot(a, low, dims)


def head_columns(ref):
    return [ref.at[:, h * DH : (h + 1) * DH] for h in range(ref.shape[1] // DH)]


def outer_kernel(a_ref, b_ref, out_ref):
    for h, (a, b) in enumerate(zip(head_columns(a_ref), head_columns(b_ref))):
        out_ref[h] = dot(a[...], b[...], TN)


def halves(rows):
    middle = rows // 2
    return [(slice(0, middle), slice(0, middle)), (slice(middle, rows), slice(0, rows))]


def masked(product):
    rows, columns = product.shape
    t = lax.broadcasted_iota(jnp.int32, product.shape, 0) + (columns - rows)
    s = lax.broadcasted_iota(jnp.int32, product.shape, 1)
    return jnp.where(s <= t, product, 0.0).astype(BF16)


def forward_kernel(q_ref, k_ref, v_ref, scale_ref, scaled_ref, intra_ref):
    scaled_ref[...] = (q_ref[...].astype(F32) * scale_ref[...]).astype(BF16)
    refs = (scaled_ref, k_ref, v_ref, intra_ref)
    for scaled, keys, values, intra in zip(*map(head_columns, refs)):
        for own, upto in halves(scaled_ref.shape[0]):
            scores = masked(dot(scaled[own], keys[upto], NT))
            intra[own] = dot(scores, values[upto], NN)


def attended_kernel(scaled_ref, intra_ref, state_ref, out_ref):
    refs = (scaled_ref, intra_ref, out_ref)
    for h, (scaled, intra, out) in enumerate(zip(*map(head_columns, refs))):
        out[...] = (split_dot(scaled[...], state_ref[h], NN) + intra[...]).astype(BF16)


def backward_kernel(
    scaled_ref, k_ref, v_ref, g_ref, scale_ref, state_ref, dq_ref, dk_ref, dv_ref
):
    rows = scaled_ref.shape[0]
    refs = (scaled_ref, k_ref, v_ref, g_ref, dq_ref, dk_ref, dv_ref)
    for h, (scaled, keys, values, grads, dq, dk, dv) in enumerate(zip(*map(head_columns, refs))):
        inter = split_dot(grads[...], state_ref[h], NT)
        for own, upto in reversed(halves(rows)):
            mixed = masked(dot(grads[own], values[upto], NT))
            scores = masked(dot(scaled[own], keys[upto], NT))
            total = inter[own] + dot(mixed, keys[upto], NN)
            dq[own] = (total * scale_ref[own]).astype(BF16)
            key_part = dot(mixed, scaled[own], TN)
            value_part = dot(scores, grads[own], TN)
            if upto.stop == rows:
                dk[...] = key_part
                dv[...] = value_part
            else:
                dk[upto] += key_part
                dv[upto] += value_part


def finish_kernel(k_ref, v_ref, dk_part_ref, dv_part_ref, after_ref, dk_ref, dv_ref):
    refs = (k_ref, v_ref, dk_part_ref, dv_part_ref, dk_ref, dv_ref)
    for h, (keys, values, dk_part, dv_part, dk, dv) in enumerate(zip(*map(head_columns, refs))):
        dk[...] = (split_dot(values[...], after_ref[h], NT) + dk_part[...]).astype(BF16)
        dv[...] = (split_dot(keys[...], after_ref[h], NN) + dv_part[...]).astype(BF16)


def per_head(kernel, rows, heads, ins, outs, macs, step=2):
    if heads % step:
        step = 1
    specs = {
        "h": pl.BlockSpec((rows, step * DH), lambda h: (0, h)),
        "v": pl.BlockSpec((rows, step * DH), lambda h: (0, h)),
        "m": pl.BlockSpec((step, DH, DH), lambda h: (h, 0, 0)),
        "s": pl.BlockSpec((rows, 1), lambda h: (0, 0)),
    }
    shapes = {"h": (rows, heads * DH), "v": (rows, heads * DH), "m": (heads, DH, DH)}
    call = pl.pallas_call(
        kernel,
        grid=(heads // step,),
        in_specs=[specs[kind] for kind in ins],
        out_specs=[specs[kind] for kind, unused in outs],
        out_shape=[
            (pltpu.HBM if kind == "h" else jax.ShapeDtypeStruct)(shapes[kind], dtype)
            for kind, dtype in outs
        ],
        compiler_params=pltpu.CompilerParams(vmem_limit_bytes=VMEM_LIMIT),
        cost_estimate=pl.CostEstimate(
            flops=2 * macs * heads,
            bytes_accessed=rows * heads * DH * 2 * (len(ins) + len(outs)),
            transcendentals=0,
        ),
    )

    def on_values(*values):
        return call(
            *[in_hbm([value])[0] if kind == "h" else value for kind, value in zip(ins, values)]
        )

    return on_values


def project_kernel(pieces, half, own_ref, other_ref, *refs):
    def fill(a_ref):
        for piece in range(pieces):
            refs[-1][piece] = dot(a_ref[...], refs[piece][...], NT).astype(BF16)

    pl.when(pl.program_id(0) < half)(lambda: fill(own_ref))
    pl.when(pl.program_id(0) >= half)(lambda: fill(other_ref))


def project(own, other, pieces):
    rows, width = own.shape
    features = pieces[0].shape[0]
    step = min(rows, 256)
    half = rows // step
    return pl.pallas_call(
        functools.partial(project_kernel, len(pieces), half),
        grid=(2 * half,),
        in_specs=[
            pl.BlockSpec((step, width), lambda r: (jnp.minimum(r, half - 1), 0)),
            pl.BlockSpec((step, width), lambda r: (jnp.maximum(r - half, 0), 0)),
        ]
        + [pl.BlockSpec((features, width), lambda r: (0, 0)) for unused in pieces],
        out_specs=pl.BlockSpec((len(pieces), step, features), lambda r: (0, r, 0)),
        out_shape=jax.ShapeDtypeStruct((len(pieces), 2 * rows, features), BF16),
        compiler_params=pltpu.CompilerParams(vmem_limit_bytes=VMEM_LIMIT),
        cost_estimate=pl.CostEstimate(
            flops=4 * rows * width * features * len(pieces),
            bytes_accessed=8 * rows * width,
            transcendentals=0,
        ),
    )(*in_hbm([own, other, *pieces]))


def products_kernel(count, late, chips, before, factor, meta_ref, *refs):
    candidates, (own_ref, other_ref), rest = refs[:count], refs[count : count + 2], refs[count + 2 :]
    weights, rest = rest[:chips], rest[chips:]
    earlier, rest = rest[:before], rest[before:]
    first_ref, second_ref, grad_ref, gathered, turned, semaphores = rest
    rows = own_ref.shape[0]
    part = weights[0].shape[0]

    @pl.when(pl.program_id(0) == 0)
    def unused():
        copies = []
        for j, candidate in enumerate(candidates):
            for u in range(candidate.shape[1] // part):
                copies.append(
                    (
                        meta_ref[2 * len(copies)] == 1,
                        pltpu.make_async_copy(
                            candidate.at[:, u * part : (u + 1) * part],
                            gathered.at[meta_ref[2 * len(copies) + 1]],
                            semaphores.at[len(copies)],
                        ),
                    )
                )
        for valid, copy in copies:
            pl.when(valid)(copy.start)
        for j in range(len(copies), len(copies) + late):

            @pl.when(meta_ref[2 * j] == 1)
            def unused_zero(j=j):
                gathered[meta_ref[2 * j + 1]] = jnp.zeros(gathered.shape[1:], BF16)

        for valid, copy in copies:
            pl.when(valid)(copy.wait)
        for delta in range(chips):
            turned[delta * part : (delta + 1) * part, :] = gathered[delta].T

    residuals = jnp.concatenate([gathered[delta] for delta in range(chips)], axis=1)
    weight = jnp.concatenate([piece[...] for piece in weights], axis=0)
    total = dot(residuals, weight, NN)
    first, second = total[:rows], total[rows:]
    if before:
        first, second = first + earlier[0][...], second + earlier[1][...]
    first_ref[...] = first
    second_ref[...] = second
    grad = dot(turned[:, :rows], own_ref[...], NN) + dot(turned[:, rows:], other_ref[...], NN)
    grad = (grad * factor).astype(BF16)
    for delta in range(chips):
        grad_ref[delta] = grad[delta * part : (delta + 1) * part]


def products(meta, candidates, late, own, other, weights, earlier, factor):
    rows, width = own.shape
    chips, part = len(weights), weights[0].shape[0]
    step = 256 if width % 256 == 0 else DH
    block = pl.BlockSpec((rows, step), lambda k, unused: (0, k))
    pieces = pl.BlockSpec((chips, part, step), lambda k, unused: (0, 0, k))
    place = jax.ShapeDtypeStruct if late else pltpu.HBM
    copies = sum(c.shape[1] for c in candidates) // part
    return pl.pallas_call(
        functools.partial(products_kernel, len(candidates), late, chips, len(earlier), factor),
        grid_spec=pltpu.PrefetchScalarGridSpec(
            num_scalar_prefetch=1,
            grid=(width // step,),
            in_specs=[pl.BlockSpec(memory_space=pltpu.HBM) for unused in candidates]
            + [block, block]
            + [pl.BlockSpec((part, step), lambda k, unused: (0, k)) for unused in weights]
            + [block for unused in earlier],
            out_specs=[block, block, pieces],
            scratch_shapes=[
                pltpu.VMEM((chips, 2 * rows, part), BF16),
                pltpu.VMEM((chips * part, 2 * rows), BF16),
                pltpu.SemaphoreType.DMA((copies,)),
            ],
        ),
        out_shape=[
            place((rows, width), F32),
            place((rows, width), F32),
            place((chips, part, width), BF16),
        ],
        compiler_params=pltpu.CompilerParams(vmem_limit_bytes=32 * rows * chips * part),
        cost_estimate=pl.CostEstimate(
            flops=8 * rows * width * part * chips,
            bytes_accessed=16 * rows * width,
            transcendentals=0,
        ),
    )(meta, *in_hbm([*candidates, own, other, *weights, *earlier]))


def late_kernel(
    chips, factor, second_type, meta_ref, piece_ref, own_ref, other_ref, first_in, second_in, grad_in, *refs
):
    weights, (first_ref, second_ref, grad_ref) = refs[:chips], refs[chips:]
    rows = own_ref.shape[0]
    valid, place = meta_ref[0] == 1, meta_ref[1]

    @pl.when(jnp.logical_not(valid))
    def unused_pass():
        first_ref[...] = first_in[...]
        second_ref[...] = second_in[...].astype(second_type)
        grad_ref[...] = grad_in[...]

    for delta, weight in enumerate(weights):

        @pl.when(valid & (place == delta))
        def unused_add(weight=weight):
            total = dot(piece_ref[...], weight[...], NN)
            first_ref[...] = first_in[...] + total[:rows]
            second_ref[...] = (second_in[...] + total[rows:]).astype(second_type)

    @pl.when(valid)
    def unused_grad():
        grad = dot(piece_ref[:rows], own_ref[...], TN) + dot(piece_ref[rows:], other_ref[...], TN)
        grad_ref[0] = (grad * factor).astype(BF16)


def late_products(meta, piece, own, other, weights, totals, grads, second_type, factor):
    rows, width = own.shape
    chips, part = len(weights), weights[0].shape[0]
    step = min(width, 512)
    block = pl.BlockSpec((rows, step), lambda k, unused: (0, k))
    slot = pl.BlockSpec((1, part, step), lambda k, meta: (meta[1], 0, k))
    return pl.pallas_call(
        functools.partial(late_kernel, chips, factor, second_type),
        grid_spec=pltpu.PrefetchScalarGridSpec(
            num_scalar_prefetch=1,
            grid=(width // step,),
            in_specs=[pl.BlockSpec(piece.shape, lambda k, unused: (0, 0)), block, block, block, block, slot]
            + [pl.BlockSpec((part, step), lambda k, unused: (0, k)) for unused in weights],
            out_specs=[block, block, slot],
        ),
        out_shape=[
            jax.ShapeDtypeStruct((rows, width), F32),
            jax.ShapeDtypeStruct((rows, width), second_type),
            jax.ShapeDtypeStruct(grads.shape, BF16),
        ],
        input_output_aliases={6: 2},
        compiler_params=pltpu.CompilerParams(vmem_limit_bytes=VMEM_LIMIT),
        cost_estimate=pl.CostEstimate(
            flops=8 * rows * width * part,
            bytes_accessed=16 * rows * width,
            transcendentals=0,
        ),
    )(meta, piece, own, other, *totals, grads, *weights)


def core_swap(value):
    count = lax.axis_size("seq")
    return lax.ppermute(value, "seq", [(j, j ^ 1) for j in range(count)])


def chip_swap(value, delta):
    count = lax.axis_size("seq")
    return lax.ppermute(value, "seq", [(j, j ^ (2 * delta)) for j in range(count)])


def line_permutes(active):
    even = [pair for pair in active if min(pair) % 2 == 0]
    odd = [pair for pair in active if min(pair) % 2 == 1]
    return even, odd


def line_step(values, active):
    return [
        lax.ppermute(value, "head", pairs) if pairs else None
        for value, pairs in zip(values, line_permutes(active))
    ]


def line_sum(part_for, beside):
    count = lax.axis_size("head")
    mine = lax.axis_index("head")
    got = [None, None]
    for step in range(1, count):
        active = [(j, j + 1) for j in range(count - 1) if j <= step - 1]
        active += [(j, j - 1) for j in range(1, count) if count - 1 - j <= step - 1]
        values = []
        for parity, pairs in enumerate(line_permutes(active)):
            if not pairs:
                values.append(None)
                continue
            target = jnp.where(mine % 2 == parity, mine + count - step, mine - count + step)
            value = part_for(jnp.clip(target, 0, count - 1))
            if step > 1 and got[1 - parity] is None:
                value, unused = lax.optimization_barrier((value, got[parity]))
            elif step > 1:
                value = (value.astype(F32) + got[1 - parity].astype(F32)).astype(BF16)
            values.append(value)
        got = line_step(values, active)
        if beside.get(step):
            got, unused = lax.optimization_barrier((got, beside[step]))
    total = part_for(mine).astype(F32)
    for value in got:
        if value is not None:
            total = total + value.astype(F32)
    return total


def line_gather(value, tied):
    tied = dict(tied)
    count = lax.axis_size("head")
    mine = lax.axis_index("head")
    found, arrived = [(value, mine >= 0, mine)], {}
    got = [value, value]
    for step in range(1, count):
        active = [(j, j + 1) for j in range(count - 1) if j >= step - 1]
        active += [(j, j - 1) for j in range(1, count) if j + step - 1 <= count - 1]
        new = line_step([value if got[1 - q] is None else got[1 - q] for q in (0, 1)], active)
        if step in tied:
            new, tied[step] = lax.optimization_barrier((new, tied[step]))
        got = new
        arrived[step] = [item for item in got if item is not None]
        for parity, item in enumerate(got):
            if item is None:
                continue
            source = jnp.where(mine % 2 == parity, mine + step, mine - step)
            found.append((item, (source >= 0) & (source < count), source))
    return found, arrived, tied


def swapped_halves(total):
    core = lax.rem(lax.axis_index("seq"), 2)
    half_heads = total.shape[0] // 2
    mine = total.astype(BF16)
    other = core_swap(mine)
    both = mine.astype(F32) + other.astype(F32)
    half = lax.dynamic_slice_in_dim(both, core * half_heads, half_heads, 0).astype(BF16)
    return half, other


def sum_of_others(half, arrived, other, lower):
    position = lax.axis_index("seq")
    chip, core = lax.div(position, 2), lax.rem(position, 2)
    summed = jnp.zeros(half.shape, F32)
    for delta, item in enumerate(arrived, 1):
        partner = chip ^ delta
        counts = (partner < chip) if lower else (partner > chip)
        summed = summed + jnp.where(counts, item.astype(F32), 0.0)
    summed = summed.astype(BF16)
    swapped = core_swap(summed)
    first = jnp.where(core == 0, summed, swapped)
    second = jnp.where(core == 0, swapped, summed)
    whole = jnp.concatenate([first, second], axis=0).astype(F32)
    return whole + jnp.where(core == (1 if lower else 0), other.astype(F32), 0.0)


def near_pieces(own):
    chips = lax.axis_size("seq") // 2
    if chips != 4:
        pieces = [own] + [chip_swap(own, delta) for delta in range(1, chips)]
        return pieces[1:], lambda arrived: [own, *arrived]
    half = own.shape[0] // 2

    def rest(arrived):
        first = chip_swap(arrived[0][:half], 2)
        second = chip_swap(arrived[1][half:], 1)
        return [own, *arrived, jnp.concatenate([first, second], axis=0)]

    return [chip_swap(own, 1), chip_swap(own, 2)], rest


def scatter_start(grads):
    chips, part = grads.shape[:2]
    if chips != 4:
        sent = [chip_swap(grads[delta], delta) for delta in range(1, chips)]
        return sent, lambda arrived: (arrived, lambda final: added(grads[0], *final))
    half = part // 2
    upper, lower = slice(0, half), slice(half, part)
    sent = [chip_swap(grads[1::2, upper], 1), chip_swap(grads[2:, lower], 2)]

    def second(arrived):
        by_x, by_y = arrived
        upper_sum = added(grads[2, upper], by_x[1]).astype(BF16)
        lower_sum = added(grads[1, lower], by_y[1]).astype(BF16)

        def finish(final):
            return jnp.concatenate(
                [
                    added(grads[0, upper], by_x[0], final[0]),
                    added(grads[0, lower], by_y[0], final[1]),
                ],
                axis=0,
            )

        return [chip_swap(upper_sum, 2), chip_swap(lower_sum, 1)], finish

    return sent, second


def added(*values):
    return sum(value.astype(F32) for value in values)


def on_device(query_rows, key_rows, value_rows, out_weight, target_rows):
    rows, width = query_rows.shape
    heads = width // DH
    groups = lax.axis_size("head")
    seq_count = lax.axis_size("seq")
    chips = seq_count // 2
    share = chips // groups
    position = lax.axis_index("seq")
    chip, core = lax.div(position, 2), lax.rem(position, 2)
    held = out_weight.shape[0]
    chunks = CHUNKS if held % (CHUNKS * DH) == 0 else 1
    part = held // chunks
    call = functools.partial(per_head, rows=rows, heads=heads)
    barrier = lax.optimization_barrier
    outer = call(outer_kernel, ins="hh", outs=[("m", F32)], macs=rows * DH * DH, step=4)

    positions = (position * rows + jnp.arange(rows, dtype=jnp.int32) + 1).astype(F32)
    scale = lax.rsqrt(F32(DH) * positions)[:, None]
    (key_value,) = outer(key_rows, value_rows)
    half, other = swapped_halves(key_value)
    half, query_rows = barrier((half, query_rows))
    arrived = [chip_swap(half, delta) for delta in range(1, chips)]
    near, rest = near_pieces(out_weight[:part])
    scaled, intra = call(
        forward_kernel, ins="hhhs", outs=[("h", BF16), ("h", F32)], macs=2 * rows * rows * DH
    )(query_rows, key_rows, value_rows, scale)
    near, scaled, intra = barrier((near, scaled, intra))
    pieces = rest(near)
    arrived, scaled = barrier((arrived, scaled))
    before = sum_of_others(half, arrived, other, True)
    (attended,) = call(
        attended_kernel, ins="hhm", outs=[("h", BF16)], macs=2 * rows * DH * DH, step=4
    )(scaled, intra, before)
    attended, pieces, target_rows = barrier((attended, pieces, target_rows))
    other_attended = core_swap(attended)

    def features_of(array, group, first, count):
        found = [
            lax.dynamic_slice_in_dim(array, (2 * j + group) * held + first, count, 1)
            for j in range(share)
        ]
        return found[0] if share == 1 else jnp.concatenate(found, axis=1)

    def chunk_of(array, c):
        found = [array[:, j * held + c * part : j * held + (c + 1) * part] for j in range(share)]
        return found[0] if share == 1 else jnp.concatenate(found, axis=1)

    other_targets = core_swap(features_of(target_rows, 1 - core, 0, held))
    targets = [
        jnp.concatenate(
            [features_of(target_rows, core, c * part, part), chunk_of(other_targets, c)], axis=0
        )
        for c in range(chunks)
    ]

    outputs, grad_parts = [], []
    gate, totals, sent, gathered = None, (), None, {}
    factor = 1.0 / math.sqrt(rows * seq_count)
    for c in range(chunks):
        last = c == chunks - 1
        if c:
            own_rows, unused = barrier((out_weight, pieces[-1]))
            near, rest = near_pieces(own_rows[c * part : (c + 1) * part])
            pieces = rest(near)
        partial_out = project(attended, other_attended, pieces)
        if gate is not None:
            partial_out, gate, outputs[-1] = barrier((partial_out, gate, outputs[-1]))

        def part_for(group, partial_out=partial_out):
            found = [
                lax.dynamic_index_in_dim(partial_out, (group * share + j) ^ chip, 0, keepdims=False)
                for j in range(share)
            ]
            return found[0] if share == 1 else jnp.concatenate(found, axis=1)

        summed = line_sum(part_for, {step - 1: items for step, items in gathered.items() if step > 1}).astype(BF16)
        residual = (summed.astype(F32) - targets[c].astype(F32)).astype(BF16)
        own_output = summed[:rows]
        other_output = core_swap(summed[rows:])
        outputs.append(
            [
                jnp.where(core == 0, own_output, other_output),
                jnp.where(core == 0, other_output, own_output),
            ]
        )
        output = None
        if last:
            output = jnp.concatenate(
                [
                    piece[group][:, j * part : (j + 1) * part]
                    for j in range(share)
                    for group in (0, 1)
                    for piece in outputs
                ],
                axis=1,
            )
        found, gathered, tied = line_gather(
            residual, {1: totals, 2: (sent, output)}
        )
        totals, (sent, output) = tied[1], tied[2]
        gate = gathered[1]
        weights = pieces
        on_time = found[:-1] if last and len(found) > 1 else found
        metas = [
            [
                value
                for j in range(share)
                for value in (
                    valid.astype(jnp.int32),
                    jnp.clip((source * share + j) ^ chip, 0, chips - 1).astype(jnp.int32),
                )
            ]
            for unused, valid, source in found
        ]
        late = found[len(on_time) :]
        if not last:
            items = [item for item, unused, unused in on_time]
            if sent is not None:
                sent, finish = second_step(sent)
                items, sent = barrier((items, sent))
                grad_parts.append(finish(sent))
        else:
            items = [item for item, unused, unused in on_time]
        *totals, grads = products(
            jnp.stack(sum(metas, [])),
            items,
            len(late) * share,
            attended,
            other_attended,
            weights,
            totals,
            factor,
        )
        if late:
            item = late[0][0]
            if sent is not None:
                sent, finish = second_step(sent)
                item, sent, totals = barrier((item, sent, totals))
                grad_parts.append(finish(sent))
            for j in range(share):
                *totals, grads = late_products(
                    jnp.stack(metas[-1][2 * j : 2 * j + 2]),
                    item[:, j * part : (j + 1) * part] if share > 1 else item,
                    attended,
                    other_attended,
                    weights,
                    totals,
                    grads,
                    BF16 if j == share - 1 else F32,
                    factor,
                )
        sent, second_step = scatter_start(grads)

    grad_attended = (totals[0] + core_swap(totals[1]).astype(F32)).astype(BF16)
    (query_grad,) = call(outer_kernel, ins="vv", outs=[("m", F32)], macs=rows * DH * DH, step=4)(
        scaled, grad_attended
    )
    half, other = swapped_halves(query_grad)
    arrived = [chip_swap(half, delta) for delta in range(1, chips)]
    grad_query, key_part, value_part = call(
        backward_kernel,
        ins="vvvvsm",
        outs=[("h", BF16), ("v", F32), ("v", F32)],
        macs=5 * rows * rows * DH,
    )(scaled, key_rows, value_rows, grad_attended, scale, before)
    arrived, key_part, value_part, grad_query, sent = barrier(
        (arrived, key_part, value_part, grad_query, sent)
    )
    sent, finish = second_step(sent)
    after = sum_of_others(half, arrived, other, False)
    grad_key, grad_value = call(
        finish_kernel, ins="vvvvm", outs=[("h", BF16), ("h", BF16)], macs=4 * rows * DH * DH
    )(key_rows, value_rows, key_part, value_part, after)
    sent, grad_key, grad_value = barrier((sent, grad_key, grad_value))
    grad_weight = jnp.concatenate([*grad_parts, finish(sent)], axis=0)
    return output, grad_query, grad_key, grad_value, grad_weight


def solution(mesh):
    placed = P("seq", "head")
    return jax.shard_map(
        on_device,
        mesh=mesh,
        in_specs=(placed,) * 5,
        out_specs=(placed,) * 5,
        check_vma=False,
    )
```

```python
import functools
import math

import jax
import jax.numpy as jnp
from jax import lax
from jax.experimental import pallas as pl
from jax.experimental.pallas import tpu as pltpu
from jax.sharding import PartitionSpec as P

DH = 128
CHUNKS = 2
F32 = jnp.float32
BF16 = jnp.bfloat16
VMEM_LIMIT = 16 * 1024 * 1024

NT = (((1,), (1,)), ((), ()))
TN = (((0,), (0,)), ((), ()))
NN = (((1,), (0,)), ((), ()))


def in_hbm(values):
    return [pltpu.with_memory_space_constraint(value, pltpu.HBM) for value in values]


def dot(a, b, dims):
    return lax.dot_general(a, b, dims, preferred_element_type=F32)


def split_dot(a, state, dims):
    high = state.astype(BF16)
    low = (state - high.astype(F32)).astype(BF16)
    return dot(a, high, dims) + dot(a, low, dims)


def head_columns(ref):
    return [ref.at[:, h * DH : (h + 1) * DH] for h in range(ref.shape[1] // DH)]


def outer_kernel(a_ref, b_ref, out_ref):
    for h, (a, b) in enumerate(zip(head_columns(a_ref), head_columns(b_ref))):
        out_ref[h] = dot(a[...], b[...], TN)


def halves(rows):
    middle = rows // 2
    return [(slice(0, middle), slice(0, middle)), (slice(middle, rows), slice(0, rows))]


def masked(product):
    rows, columns = product.shape
    t = lax.broadcasted_iota(jnp.int32, product.shape, 0) + (columns - rows)
    s = lax.broadcasted_iota(jnp.int32, product.shape, 1)
    return jnp.where(s <= t, product, 0.0).astype(BF16)


def forward_kernel(q_ref, k_ref, v_ref, scale_ref, scaled_ref, intra_ref):
    scaled_ref[...] = (q_ref[...].astype(F32) * scale_ref[...]).astype(BF16)
    refs = (scaled_ref, k_ref, v_ref, intra_ref)
    for scaled, keys, values, intra in zip(*map(head_columns, refs)):
        for own, upto in halves(scaled_ref.shape[0]):
            scores = masked(dot(scaled[own], keys[upto], NT))
            intra[own] = dot(scores, values[upto], NN)


def attended_kernel(scaled_ref, intra_ref, state_ref, out_ref):
    refs = (scaled_ref, intra_ref, out_ref)
    for h, (scaled, intra, out) in enumerate(zip(*map(head_columns, refs))):
        out[...] = (split_dot(scaled[...], state_ref[h], NN) + intra[...]).astype(BF16)


def backward_kernel(
    scaled_ref, k_ref, v_ref, g_ref, scale_ref, state_ref, dq_ref, dk_ref, dv_ref
):
    rows = scaled_ref.shape[0]
    refs = (scaled_ref, k_ref, v_ref, g_ref, dq_ref, dk_ref, dv_ref)
    for h, (scaled, keys, values, grads, dq, dk, dv) in enumerate(zip(*map(head_columns, refs))):
        inter = split_dot(grads[...], state_ref[h], NT)
        for own, upto in reversed(halves(rows)):
            mixed = masked(dot(grads[own], values[upto], NT))
            scores = masked(dot(scaled[own], keys[upto], NT))
            total = inter[own] + dot(mixed, keys[upto], NN)
            dq[own] = (total * scale_ref[own]).astype(BF16)
            key_part = dot(mixed, scaled[own], TN)
            value_part = dot(scores, grads[own], TN)
            if upto.stop == rows:
                dk[...] = key_part
                dv[...] = value_part
            else:
                dk[upto] += key_part
                dv[upto] += value_part


def finish_kernel(k_ref, v_ref, dk_part_ref, dv_part_ref, after_ref, dk_ref, dv_ref):
    refs = (k_ref, v_ref, dk_part_ref, dv_part_ref, dk_ref, dv_ref)
    for h, (keys, values, dk_part, dv_part, dk, dv) in enumerate(zip(*map(head_columns, refs))):
        dk[...] = (split_dot(values[...], after_ref[h], NT) + dk_part[...]).astype(BF16)
        dv[...] = (split_dot(keys[...], after_ref[h], NN) + dv_part[...]).astype(BF16)


def per_head(kernel, rows, heads, ins, outs, macs, step=2):
    if heads % step:
        step = 1
    specs = {
        "h": pl.BlockSpec((rows, step * DH), lambda h: (0, h)),
        "v": pl.BlockSpec((rows, step * DH), lambda h: (0, h)),
        "m": pl.BlockSpec((step, DH, DH), lambda h: (h, 0, 0)),
        "s": pl.BlockSpec((rows, 1), lambda h: (0, 0)),
    }
    shapes = {"h": (rows, heads * DH), "v": (rows, heads * DH), "m": (heads, DH, DH)}
    call = pl.pallas_call(
        kernel,
        grid=(heads // step,),
        in_specs=[specs[kind] for kind in ins],
        out_specs=[specs[kind] for kind, unused in outs],
        out_shape=[
            (pltpu.HBM if kind == "h" else jax.ShapeDtypeStruct)(shapes[kind], dtype)
            for kind, dtype in outs
        ],
        compiler_params=pltpu.CompilerParams(vmem_limit_bytes=VMEM_LIMIT),
        cost_estimate=pl.CostEstimate(
            flops=2 * macs * heads,
            bytes_accessed=rows * heads * DH * 2 * (len(ins) + len(outs)),
            transcendentals=0,
        ),
    )

    def on_values(*values):
        return call(
            *[in_hbm([value])[0] if kind == "h" else value for kind, value in zip(ins, values)]
        )

    return on_values


def project_kernel(pieces, a_ref, *refs):
    for piece in range(pieces):
        refs[-1][piece] = dot(a_ref[...], refs[piece][...], NT).astype(BF16)


def project_rows(attended, pieces, half, into):
    rows, width = attended.shape
    features = pieces[0].shape[0]
    step = min(rows, 256)
    first = half * (rows // step)
    more = [] if into is None else [into]
    return pl.pallas_call(
        functools.partial(project_kernel, len(pieces)),
        grid=(rows // step,),
        in_specs=[pl.BlockSpec((step, width), lambda r: (r, 0))]
        + [pl.BlockSpec((features, width), lambda r: (0, 0)) for unused in pieces]
        + [pl.BlockSpec(memory_space=pl.ANY) for unused in more],
        out_specs=pl.BlockSpec((len(pieces), step, features), lambda r: (0, r + first, 0)),
        out_shape=jax.ShapeDtypeStruct((len(pieces), 2 * rows, features), BF16),
        input_output_aliases={len(pieces) + 1: 0} if more else {},
        compiler_params=pltpu.CompilerParams(vmem_limit_bytes=VMEM_LIMIT),
        cost_estimate=pl.CostEstimate(
            flops=2 * rows * width * features * len(pieces),
            bytes_accessed=4 * rows * width,
            transcendentals=0,
        ),
    )(*([attended] if more else in_hbm([attended])), *in_hbm(pieces), *more)


def project(own, other, pieces):
    return project_rows(other, pieces, 1, project_rows(own, pieces, 0, None))


def products_kernel(count, late, chips, before, factor, meta_ref, *refs):
    candidates, (own_ref, other_ref), rest = refs[:count], refs[count : count + 2], refs[count + 2 :]
    weights, rest = rest[:chips], rest[chips:]
    earlier, rest = rest[:before], rest[before:]
    first_ref, second_ref, grad_ref, gathered, turned, semaphores = rest
    rows = own_ref.shape[0]
    part = weights[0].shape[0]

    @pl.when(pl.program_id(0) == 0)
    def unused():
        copies = []
        for j, candidate in enumerate(candidates):
            for u in range(candidate.shape[1] // part):
                copies.append(
                    (
                        meta_ref[2 * len(copies)] == 1,
                        pltpu.make_async_copy(
                            candidate.at[:, u * part : (u + 1) * part],
                            gathered.at[meta_ref[2 * len(copies) + 1]],
                            semaphores.at[len(copies)],
                        ),
                    )
                )
        for valid, copy in copies:
            pl.when(valid)(copy.start)
        for j in range(len(copies), len(copies) + late):

            @pl.when(meta_ref[2 * j] == 1)
            def unused_zero(j=j):
                gathered[meta_ref[2 * j + 1]] = jnp.zeros(gathered.shape[1:], BF16)

        for valid, copy in copies:
            pl.when(valid)(copy.wait)
        for delta in range(chips):
            turned[delta * part : (delta + 1) * part, :] = gathered[delta].T

    residuals = jnp.concatenate([gathered[delta] for delta in range(chips)], axis=1)
    weight = jnp.concatenate([piece[...] for piece in weights], axis=0)
    total = dot(residuals, weight, NN)
    first, second = total[:rows], total[rows:]
    if before:
        first, second = first + earlier[0][...], second + earlier[1][...]
    first_ref[...] = first
    second_ref[...] = second
    grad = dot(turned[:, :rows], own_ref[...], NN) + dot(turned[:, rows:], other_ref[...], NN)
    grad = (grad * factor).astype(BF16)
    for delta in range(chips):
        grad_ref[delta] = grad[delta * part : (delta + 1) * part]


def products(meta, candidates, late, own, other, weights, earlier, factor):
    rows, width = own.shape
    chips, part = len(weights), weights[0].shape[0]
    step = 256 if width % 256 == 0 else DH
    block = pl.BlockSpec((rows, step), lambda k, unused: (0, k))
    pieces = pl.BlockSpec((chips, part, step), lambda k, unused: (0, 0, k))
    place = jax.ShapeDtypeStruct if late else pltpu.HBM
    copies = sum(c.shape[1] for c in candidates) // part
    return pl.pallas_call(
        functools.partial(products_kernel, len(candidates), late, chips, len(earlier), factor),
        grid_spec=pltpu.PrefetchScalarGridSpec(
            num_scalar_prefetch=1,
            grid=(width // step,),
            in_specs=[pl.BlockSpec(memory_space=pltpu.HBM) for unused in candidates]
            + [block, block]
            + [pl.BlockSpec((part, step), lambda k, unused: (0, k)) for unused in weights]
            + [block for unused in earlier],
            out_specs=[block, block, pieces],
            scratch_shapes=[
                pltpu.VMEM((chips, 2 * rows, part), BF16),
                pltpu.VMEM((chips * part, 2 * rows), BF16),
                pltpu.SemaphoreType.DMA((copies,)),
            ],
        ),
        out_shape=[
            place((rows, width), F32),
            place((rows, width), F32),
            place((chips, part, width), BF16),
        ],
        compiler_params=pltpu.CompilerParams(vmem_limit_bytes=32 * rows * chips * part),
        cost_estimate=pl.CostEstimate(
            flops=8 * rows * width * part * chips,
            bytes_accessed=16 * rows * width,
            transcendentals=0,
        ),
    )(meta, *in_hbm([*candidates, own, other, *weights, *earlier]))


def late_kernel(
    chips, factor, second_type, meta_ref, piece_ref, own_ref, other_ref, first_in, second_in, grad_in, *refs
):
    weights, (first_ref, second_ref, grad_ref) = refs[:chips], refs[chips:]
    rows = own_ref.shape[0]
    valid, place = meta_ref[0] == 1, meta_ref[1]

    @pl.when(jnp.logical_not(valid))
    def unused_pass():
        first_ref[...] = first_in[...]
        second_ref[...] = second_in[...].astype(second_type)
        grad_ref[...] = grad_in[...]

    for delta, weight in enumerate(weights):

        @pl.when(valid & (place == delta))
        def unused_add(weight=weight):
            total = dot(piece_ref[...], weight[...], NN)
            first_ref[...] = first_in[...] + total[:rows]
            second_ref[...] = (second_in[...] + total[rows:]).astype(second_type)

    @pl.when(valid)
    def unused_grad():
        grad = dot(piece_ref[:rows], own_ref[...], TN) + dot(piece_ref[rows:], other_ref[...], TN)
        grad_ref[0] = (grad * factor).astype(BF16)


def late_products(meta, piece, own, other, weights, totals, grads, second_type, factor):
    rows, width = own.shape
    chips, part = len(weights), weights[0].shape[0]
    step = min(width, 512)
    block = pl.BlockSpec((rows, step), lambda k, unused: (0, k))
    slot = pl.BlockSpec((1, part, step), lambda k, meta: (meta[1], 0, k))
    return pl.pallas_call(
        functools.partial(late_kernel, chips, factor, second_type),
        grid_spec=pltpu.PrefetchScalarGridSpec(
            num_scalar_prefetch=1,
            grid=(width // step,),
            in_specs=[pl.BlockSpec(piece.shape, lambda k, unused: (0, 0)), block, block, block, block, slot]
            + [pl.BlockSpec((part, step), lambda k, unused: (0, k)) for unused in weights],
            out_specs=[block, block, slot],
        ),
        out_shape=[
            jax.ShapeDtypeStruct((rows, width), F32),
            jax.ShapeDtypeStruct((rows, width), second_type),
            jax.ShapeDtypeStruct(grads.shape, BF16),
        ],
        input_output_aliases={6: 2},
        compiler_params=pltpu.CompilerParams(vmem_limit_bytes=VMEM_LIMIT),
        cost_estimate=pl.CostEstimate(
            flops=8 * rows * width * part,
            bytes_accessed=16 * rows * width,
            transcendentals=0,
        ),
    )(meta, piece, own, other, *totals, grads, *weights)


def core_swap(value):
    count = lax.axis_size("seq")
    return lax.ppermute(value, "seq", [(j, j ^ 1) for j in range(count)])


def chip_swap(value, delta):
    count = lax.axis_size("seq")
    return lax.ppermute(value, "seq", [(j, j ^ (2 * delta)) for j in range(count)])


def line_permutes(active):
    even = [pair for pair in active if min(pair) % 2 == 0]
    odd = [pair for pair in active if min(pair) % 2 == 1]
    return even, odd


def line_step(values, active):
    return [
        lax.ppermute(value, "head", pairs) if pairs else None
        for value, pairs in zip(values, line_permutes(active))
    ]


def line_sum(part_for, beside):
    count = lax.axis_size("head")
    mine = lax.axis_index("head")
    got = [None, None]
    for step in range(1, count):
        active = [(j, j + 1) for j in range(count - 1) if j <= step - 1]
        active += [(j, j - 1) for j in range(1, count) if count - 1 - j <= step - 1]
        values = []
        for parity, pairs in enumerate(line_permutes(active)):
            if not pairs:
                values.append(None)
                continue
            target = jnp.where(mine % 2 == parity, mine + count - step, mine - count + step)
            value = part_for(jnp.clip(target, 0, count - 1))
            if got[1 - parity] is not None:
                value = (value.astype(F32) + got[1 - parity].astype(F32)).astype(BF16)
            values.append(value)
        got = line_step(values, active)
        if beside.get(step):
            got, unused = lax.optimization_barrier((got, beside[step]))
    total = part_for(mine).astype(F32)
    for value in got:
        if value is not None:
            total = total + value.astype(F32)
    return total


def line_gather(value, tied):
    tied = dict(tied)
    count = lax.axis_size("head")
    mine = lax.axis_index("head")
    found, arrived = [(value, mine >= 0, mine)], {}
    got = [value, value]
    for step in range(1, count):
        active = [(j, j + 1) for j in range(count - 1) if j >= step - 1]
        active += [(j, j - 1) for j in range(1, count) if j + step - 1 <= count - 1]
        new = line_step([value if got[1 - q] is None else got[1 - q] for q in (0, 1)], active)
        if step in tied:
            new, tied[step] = lax.optimization_barrier((new, tied[step]))
        got = new
        arrived[step] = [item for item in got if item is not None]
        for parity, item in enumerate(got):
            if item is None:
                continue
            source = jnp.where(mine % 2 == parity, mine + step, mine - step)
            found.append((item, (source >= 0) & (source < count), source))
    return found, arrived, tied


def swapped_halves(total):
    core = lax.rem(lax.axis_index("seq"), 2)
    half_heads = total.shape[0] // 2
    mine = total.astype(BF16)
    other = core_swap(mine)
    both = mine.astype(F32) + other.astype(F32)
    half = lax.dynamic_slice_in_dim(both, core * half_heads, half_heads, 0).astype(BF16)
    return half, other


def sum_of_others(half, arrived, other, lower):
    position = lax.axis_index("seq")
    chip, core = lax.div(position, 2), lax.rem(position, 2)
    summed = jnp.zeros(half.shape, F32)
    for delta, item in enumerate(arrived, 1):
        partner = chip ^ delta
        counts = (partner < chip) if lower else (partner > chip)
        summed = summed + jnp.where(counts, item.astype(F32), 0.0)
    summed = summed.astype(BF16)
    swapped = core_swap(summed)
    first = jnp.where(core == 0, summed, swapped)
    second = jnp.where(core == 0, swapped, summed)
    whole = jnp.concatenate([first, second], axis=0).astype(F32)
    return whole + jnp.where(core == (1 if lower else 0), other.astype(F32), 0.0)


def near_pieces(own):
    chips = lax.axis_size("seq") // 2
    if chips != 4:
        pieces = [own] + [chip_swap(own, delta) for delta in range(1, chips)]
        return pieces[1:], lambda arrived: [own, *arrived]
    half = own.shape[0] // 2

    def rest(arrived):
        first = chip_swap(arrived[0][:half], 2)
        second = chip_swap(arrived[1][half:], 1)
        return [own, *arrived, jnp.concatenate([first, second], axis=0)]

    return [chip_swap(own, 1), chip_swap(own, 2)], rest


def scatter_start(grads):
    chips, part = grads.shape[:2]
    if chips != 4:
        sent = [chip_swap(grads[delta], delta) for delta in range(1, chips)]
        return sent, lambda arrived: (arrived, lambda final: added(grads[0], *final))
    half = part // 2
    upper, lower = slice(0, half), slice(half, part)
    sent = [chip_swap(grads[1::2, upper], 1), chip_swap(grads[2:, lower], 2)]

    def second(arrived):
        by_x, by_y = arrived
        upper_sum = added(grads[2, upper], by_x[1]).astype(BF16)
        lower_sum = added(grads[1, lower], by_y[1]).astype(BF16)

        def finish(final):
            return jnp.concatenate(
                [
                    added(grads[0, upper], by_x[0], final[0]),
                    added(grads[0, lower], by_y[0], final[1]),
                ],
                axis=0,
            )

        return [chip_swap(upper_sum, 2), chip_swap(lower_sum, 1)], finish

    return sent, second


def added(*values):
    return sum(value.astype(F32) for value in values)


def on_device(query_rows, key_rows, value_rows, out_weight, target_rows):
    rows, width = query_rows.shape
    heads = width // DH
    groups = lax.axis_size("head")
    seq_count = lax.axis_size("seq")
    chips = seq_count // 2
    share = chips // groups
    position = lax.axis_index("seq")
    chip, core = lax.div(position, 2), lax.rem(position, 2)
    held = out_weight.shape[0]
    chunks = CHUNKS if held % (CHUNKS * DH) == 0 else 1
    part = held // chunks
    call = functools.partial(per_head, rows=rows, heads=heads)
    barrier = lax.optimization_barrier
    outer = call(outer_kernel, ins="hh", outs=[("m", F32)], macs=rows * DH * DH, step=4)

    positions = (position * rows + jnp.arange(rows, dtype=jnp.int32) + 1).astype(F32)
    scale = lax.rsqrt(F32(DH) * positions)[:, None]
    (key_value,) = outer(key_rows, value_rows)
    half, other = swapped_halves(key_value)
    half, query_rows = barrier((half, query_rows))
    arrived = [chip_swap(half, delta) for delta in range(1, chips)]
    near, rest = near_pieces(out_weight[:part])
    scaled, intra = call(
        forward_kernel, ins="hhhs", outs=[("h", BF16), ("h", F32)], macs=2 * rows * rows * DH
    )(query_rows, key_rows, value_rows, scale)
    near, scaled, intra = barrier((near, scaled, intra))
    pieces = rest(near)
    arrived, scaled = barrier((arrived, scaled))
    before = sum_of_others(half, arrived, other, True)
    (attended,) = call(
        attended_kernel, ins="hhm", outs=[("h", BF16)], macs=2 * rows * DH * DH, step=4
    )(scaled, intra, before)
    attended, pieces, target_rows = barrier((attended, pieces, target_rows))
    other_attended = core_swap(attended)

    def features_of(array, group, first, count):
        found = [
            lax.dynamic_slice_in_dim(array, (2 * j + group) * held + first, count, 1)
            for j in range(share)
        ]
        return found[0] if share == 1 else jnp.concatenate(found, axis=1)

    def chunk_of(array, c):
        found = [array[:, j * held + c * part : j * held + (c + 1) * part] for j in range(share)]
        return found[0] if share == 1 else jnp.concatenate(found, axis=1)

    other_targets = core_swap(features_of(target_rows, 1 - core, 0, held))
    targets = [
        jnp.concatenate(
            [features_of(target_rows, core, c * part, part), chunk_of(other_targets, c)], axis=0
        )
        for c in range(chunks)
    ]

    outputs, grad_parts = [], []
    gate, totals, sent, pending, gathered = None, (), None, None, {}
    factor = 1.0 / math.sqrt(rows * seq_count)
    for c in range(chunks):
        last = c == chunks - 1
        if c:
            own_rows, unused = barrier((out_weight, pieces[-1]))
            near, rest = near_pieces(own_rows[c * part : (c + 1) * part])
            pieces = rest(near)
        partial_out = project(attended, other_attended, pieces)
        if gate is not None:
            partial_out, gate, outputs[-1] = barrier((partial_out, gate, outputs[-1]))

        def part_for(group, partial_out=partial_out):
            found = [
                lax.dynamic_index_in_dim(partial_out, (group * share + j) ^ chip, 0, keepdims=False)
                for j in range(share)
            ]
            return found[0] if share == 1 else jnp.concatenate(found, axis=1)

        summed = line_sum(part_for, {step - 1: items for step, items in gathered.items() if step > 1}).astype(BF16)
        residual = (summed.astype(F32) - targets[c].astype(F32)).astype(BF16)
        own_output = summed[:rows]
        other_output = core_swap(summed[rows:])
        outputs.append(
            [
                jnp.where(core == 0, own_output, other_output),
                jnp.where(core == 0, other_output, own_output),
            ]
        )
        output = None
        if last:
            output = jnp.concatenate(
                [
                    piece[group][:, j * part : (j + 1) * part]
                    for j in range(share)
                    for group in (0, 1)
                    for piece in outputs
                ],
                axis=1,
            )
        if pending is not None:
            pending, output = barrier((pending, output))
            sent, second_step = scatter_start(pending)
        found, gathered, tied = line_gather(
            residual, {1: totals, 2: output}
        )
        totals, output = tied[1], tied[2]
        gate = residual
        weights = pieces
        on_time = found[:-1] if last and len(found) > 1 else found
        metas = [
            [
                value
                for j in range(share)
                for value in (
                    valid.astype(jnp.int32),
                    jnp.clip((source * share + j) ^ chip, 0, chips - 1).astype(jnp.int32),
                )
            ]
            for unused, valid, source in found
        ]
        late = found[len(on_time) :]
        if not last:
            items = [item for item, unused, unused in on_time]
            if sent is not None:
                sent, finish = second_step(sent)
                items, sent = barrier((items, sent))
                grad_parts.append(finish(sent))
        else:
            items = [item for item, unused, unused in on_time]
        *totals, grads = products(
            jnp.stack(sum(metas, [])),
            items,
            len(late) * share,
            attended,
            other_attended,
            weights,
            totals,
            factor,
        )
        if late:
            item = late[0][0]
            if sent is not None:
                sent, finish = second_step(sent)
                item, sent, totals = barrier((item, sent, totals))
                grad_parts.append(finish(sent))
            for j in range(share):
                *totals, grads = late_products(
                    jnp.stack(metas[-1][2 * j : 2 * j + 2]),
                    item[:, j * part : (j + 1) * part] if share > 1 else item,
                    attended,
                    other_attended,
                    weights,
                    totals,
                    grads,
                    BF16 if j == share - 1 else F32,
                    factor,
                )
        pending = grads

    sent, second_step = scatter_start(pending)
    grad_attended = (totals[0] + core_swap(totals[1]).astype(F32)).astype(BF16)
    (query_grad,) = call(outer_kernel, ins="vv", outs=[("m", F32)], macs=rows * DH * DH, step=4)(
        scaled, grad_attended
    )
    half, other = swapped_halves(query_grad)
    arrived = [chip_swap(half, delta) for delta in range(1, chips)]
    grad_query, key_part, value_part = call(
        backward_kernel,
        ins="vvvvsm",
        outs=[("h", BF16), ("v", F32), ("v", F32)],
        macs=5 * rows * rows * DH,
    )(scaled, key_rows, value_rows, grad_attended, scale, before)
    arrived, key_part, value_part, grad_query, sent = barrier(
        (arrived, key_part, value_part, grad_query, sent)
    )
    sent, finish = second_step(sent)
    after = sum_of_others(half, arrived, other, False)
    grad_key, grad_value = call(
        finish_kernel, ins="vvvvm", outs=[("h", BF16), ("h", BF16)], macs=4 * rows * DH * DH
    )(key_rows, value_rows, key_part, value_part, after)
    sent, grad_key, grad_value = barrier((sent, grad_key, grad_value))
    grad_weight = jnp.concatenate([*grad_parts, finish(sent)], axis=0)
    return output, grad_query, grad_key, grad_value, grad_weight


def solution(mesh):
    placed = P("seq", "head")
    return jax.shard_map(
        on_device,
        mesh=mesh,
        in_specs=(placed,) * 5,
        out_specs=(placed,) * 5,
        check_vma=False,
    )
```

```python
import functools
import math

import jax
import jax.numpy as jnp
from jax import lax
from jax.experimental import pallas as pl
from jax.experimental.pallas import tpu as pltpu
from jax.sharding import PartitionSpec as P

DH = 128
CHUNKS = 2
F32 = jnp.float32
BF16 = jnp.bfloat16
VMEM_LIMIT = 12 * 1024 * 1024

NT = (((1,), (1,)), ((), ()))
TN = (((0,), (0,)), ((), ()))
NN = (((1,), (0,)), ((), ()))


def in_hbm(values):
    return [pltpu.with_memory_space_constraint(value, pltpu.HBM) for value in values]


def dot(a, b, dims):
    return lax.dot_general(a, b, dims, preferred_element_type=F32)


def split_dot(a, state, dims):
    high = state.astype(BF16)
    low = (state - high.astype(F32)).astype(BF16)
    return dot(a, high, dims) + dot(a, low, dims)


def head_columns(ref):
    return [ref.at[:, h * DH : (h + 1) * DH] for h in range(ref.shape[1] // DH)]


def outer_kernel(a_ref, b_ref, out_ref):
    for h, (a, b) in enumerate(zip(head_columns(a_ref), head_columns(b_ref))):
        out_ref[h] = dot(a[...], b[...], TN)


def halves(rows):
    middle = rows // 2
    return [(slice(0, middle), slice(0, middle)), (slice(middle, rows), slice(0, rows))]


def masked(product):
    rows, columns = product.shape
    t = lax.broadcasted_iota(jnp.int32, product.shape, 0) + (columns - rows)
    s = lax.broadcasted_iota(jnp.int32, product.shape, 1)
    return jnp.where(s <= t, product, 0.0).astype(BF16)


def forward_kernel(q_ref, k_ref, v_ref, scale_ref, scaled_ref, intra_ref):
    scaled_ref[...] = (q_ref[...].astype(F32) * scale_ref[...]).astype(BF16)
    refs = (scaled_ref, k_ref, v_ref, intra_ref)
    for scaled, keys, values, intra in zip(*map(head_columns, refs)):
        for own, upto in halves(scaled_ref.shape[0]):
            scores = masked(dot(scaled[own], keys[upto], NT))
            intra[own] = dot(scores, values[upto], NN)


def attended_kernel(scaled_ref, intra_ref, state_ref, out_ref):
    refs = (scaled_ref, intra_ref, out_ref)
    for h, (scaled, intra, out) in enumerate(zip(*map(head_columns, refs))):
        out[...] = (split_dot(scaled[...], state_ref[h], NN) + intra[...]).astype(BF16)


def backward_kernel(
    scaled_ref, k_ref, v_ref, g_ref, scale_ref, state_ref, dq_ref, dk_ref, dv_ref
):
    rows = scaled_ref.shape[0]
    refs = (scaled_ref, k_ref, v_ref, g_ref, dq_ref, dk_ref, dv_ref)
    for h, (scaled, keys, values, grads, dq, dk, dv) in enumerate(zip(*map(head_columns, refs))):
        inter = split_dot(grads[...], state_ref[h], NT)
        for own, upto in reversed(halves(rows)):
            mixed = masked(dot(grads[own], values[upto], NT))
            scores = masked(dot(scaled[own], keys[upto], NT))
            total = inter[own] + dot(mixed, keys[upto], NN)
            dq[own] = (total * scale_ref[own]).astype(BF16)
            key_part = dot(mixed, scaled[own], TN)
            value_part = dot(scores, grads[own], TN)
            if upto.stop == rows:
                dk[...] = key_part
                dv[...] = value_part
            else:
                dk[upto] += key_part
                dv[upto] += value_part


def finish_kernel(k_ref, v_ref, dk_part_ref, dv_part_ref, after_ref, dk_ref, dv_ref):
    refs = (k_ref, v_ref, dk_part_ref, dv_part_ref, dk_ref, dv_ref)
    for h, (keys, values, dk_part, dv_part, dk, dv) in enumerate(zip(*map(head_columns, refs))):
        dk[...] = (split_dot(values[...], after_ref[h], NT) + dk_part[...]).astype(BF16)
        dv[...] = (split_dot(keys[...], after_ref[h], NN) + dv_part[...]).astype(BF16)


def per_head(kernel, rows, heads, ins, outs, macs, step=2):
    if heads % step:
        step = 1
    specs = {
        "h": pl.BlockSpec((rows, step * DH), lambda h: (0, h)),
        "v": pl.BlockSpec((rows, step * DH), lambda h: (0, h)),
        "m": pl.BlockSpec((step, DH, DH), lambda h: (h, 0, 0)),
        "s": pl.BlockSpec((rows, 1), lambda h: (0, 0)),
    }
    shapes = {"h": (rows, heads * DH), "v": (rows, heads * DH), "m": (heads, DH, DH)}
    call = pl.pallas_call(
        kernel,
        grid=(heads // step,),
        in_specs=[specs[kind] for kind in ins],
        out_specs=[specs[kind] for kind, unused in outs],
        out_shape=[
            (pltpu.HBM if kind == "h" else jax.ShapeDtypeStruct)(shapes[kind], dtype)
            for kind, dtype in outs
        ],
        compiler_params=pltpu.CompilerParams(vmem_limit_bytes=VMEM_LIMIT // 2),
        cost_estimate=pl.CostEstimate(
            flops=2 * macs * heads,
            bytes_accessed=rows * heads * DH * 2 * (len(ins) + len(outs)),
            transcendentals=0,
        ),
    )

    def on_values(*values):
        return call(
            *[in_hbm([value])[0] if kind == "h" else value for kind, value in zip(ins, values)]
        )

    return on_values


def project_kernel(pieces, a_ref, *refs):
    for piece in range(pieces):
        refs[-1][piece] = dot(a_ref[...], refs[piece][...], NT).astype(BF16)


def project_rows(attended, pieces, half, into):
    rows, width = attended.shape
    features = pieces[0].shape[0]
    step = min(rows, 256)
    first = half * (rows // step)
    more = [] if into is None else [into]
    return pl.pallas_call(
        functools.partial(project_kernel, len(pieces)),
        grid=(rows // step,),
        in_specs=[pl.BlockSpec((step, width), lambda r: (r, 0))]
        + [pl.BlockSpec((features, width), lambda r: (0, 0)) for unused in pieces]
        + [pl.BlockSpec(memory_space=pl.ANY) for unused in more],
        out_specs=pl.BlockSpec((len(pieces), step, features), lambda r: (0, r + first, 0)),
        out_shape=jax.ShapeDtypeStruct((len(pieces), 2 * rows, features), BF16),
        input_output_aliases={len(pieces) + 1: 0} if more else {},
        compiler_params=pltpu.CompilerParams(vmem_limit_bytes=VMEM_LIMIT),
        cost_estimate=pl.CostEstimate(
            flops=2 * rows * width * features * len(pieces),
            bytes_accessed=4 * rows * width,
            transcendentals=0,
        ),
    )(*([attended] if more else in_hbm([attended])), *in_hbm(pieces), *more)


def project(own, other, pieces):
    return project_rows(other, pieces, 1, project_rows(own, pieces, 0, None))


def products_kernel(count, late, chips, before, factor, meta_ref, *refs):
    candidates, (own_ref, other_ref), rest = refs[:count], refs[count : count + 2], refs[count + 2 :]
    weights, rest = rest[:chips], rest[chips:]
    earlier, rest = rest[:before], rest[before:]
    first_ref, second_ref, grad_ref, gathered, turned, semaphores = rest
    rows = own_ref.shape[0]
    part = weights[0].shape[0]

    @pl.when(pl.program_id(0) == 0)
    def unused():
        copies = []
        for j, candidate in enumerate(candidates):
            for u in range(candidate.shape[1] // part):
                copies.append(
                    (
                        meta_ref[2 * len(copies)] == 1,
                        pltpu.make_async_copy(
                            candidate.at[:, u * part : (u + 1) * part],
                            gathered.at[meta_ref[2 * len(copies) + 1]],
                            semaphores.at[len(copies)],
                        ),
                    )
                )
        for valid, copy in copies:
            pl.when(valid)(copy.start)
        for j in range(len(copies), len(copies) + late):

            @pl.when(meta_ref[2 * j] == 1)
            def unused_zero(j=j):
                gathered[meta_ref[2 * j + 1]] = jnp.zeros(gathered.shape[1:], BF16)

        for valid, copy in copies:
            pl.when(valid)(copy.wait)
        for delta in range(chips):
            turned[delta * part : (delta + 1) * part, :] = gathered[delta].T

    residuals = jnp.concatenate([gathered[delta] for delta in range(chips)], axis=1)
    weight = jnp.concatenate([piece[...] for piece in weights], axis=0)
    total = dot(residuals, weight, NN)
    first, second = total[:rows], total[rows:]
    if before:
        first, second = first + earlier[0][...], second + earlier[1][...]
    first_ref[...] = first
    second_ref[...] = second
    grad = dot(turned[:, :rows], own_ref[...], NN) + dot(turned[:, rows:], other_ref[...], NN)
    grad = (grad * factor).astype(BF16)
    for delta in range(chips):
        grad_ref[delta] = grad[delta * part : (delta + 1) * part]


def products(meta, candidates, late, own, other, weights, earlier, factor):
    rows, width = own.shape
    chips, part = len(weights), weights[0].shape[0]
    step = 256 if width % 256 == 0 else DH
    block = pl.BlockSpec((rows, step), lambda k, unused: (0, k))
    pieces = pl.BlockSpec((chips, part, step), lambda k, unused: (0, 0, k))
    place = jax.ShapeDtypeStruct if late else pltpu.HBM
    copies = sum(c.shape[1] for c in candidates) // part
    return pl.pallas_call(
        functools.partial(products_kernel, len(candidates), late, chips, len(earlier), factor),
        grid_spec=pltpu.PrefetchScalarGridSpec(
            num_scalar_prefetch=1,
            grid=(width // step,),
            in_specs=[pl.BlockSpec(memory_space=pltpu.HBM) for unused in candidates]
            + [block, block]
            + [pl.BlockSpec((part, step), lambda k, unused: (0, k)) for unused in weights]
            + [block for unused in earlier],
            out_specs=[block, block, pieces],
            scratch_shapes=[
                pltpu.VMEM((chips, 2 * rows, part), BF16),
                pltpu.VMEM((chips * part, 2 * rows), BF16),
                pltpu.SemaphoreType.DMA((copies,)),
            ],
        ),
        out_shape=[
            place((rows, width), F32),
            place((rows, width), F32),
            place((chips, part, width), BF16),
        ],
        compiler_params=pltpu.CompilerParams(vmem_limit_bytes=24 * rows * chips * part),
        cost_estimate=pl.CostEstimate(
            flops=8 * rows * width * part * chips,
            bytes_accessed=16 * rows * width,
            transcendentals=0,
        ),
    )(meta, *in_hbm([*candidates, own, other, *weights, *earlier]))


def late_kernel(
    chips, factor, second_type, meta_ref, piece_ref, own_ref, other_ref, first_in, second_in, grad_in, *refs
):
    weights, (first_ref, second_ref, grad_ref) = refs[:chips], refs[chips:]
    rows = own_ref.shape[0]
    valid, place = meta_ref[0] == 1, meta_ref[1]

    @pl.when(jnp.logical_not(valid))
    def unused_pass():
        first_ref[...] = first_in[...]
        second_ref[...] = second_in[...].astype(second_type)
        grad_ref[...] = grad_in[...]

    for delta, weight in enumerate(weights):

        @pl.when(valid & (place == delta))
        def unused_add(weight=weight):
            total = dot(piece_ref[...], weight[...], NN)
            first_ref[...] = first_in[...] + total[:rows]
            second_ref[...] = (second_in[...] + total[rows:]).astype(second_type)

    @pl.when(valid)
    def unused_grad():
        grad = dot(piece_ref[:rows], own_ref[...], TN) + dot(piece_ref[rows:], other_ref[...], TN)
        grad_ref[0] = (grad * factor).astype(BF16)


def late_products(meta, piece, own, other, weights, totals, grads, second_type, factor):
    rows, width = own.shape
    chips, part = len(weights), weights[0].shape[0]
    step = min(width, 512)
    block = pl.BlockSpec((rows, step), lambda k, unused: (0, k))
    slot = pl.BlockSpec((1, part, step), lambda k, meta: (meta[1], 0, k))
    return pl.pallas_call(
        functools.partial(late_kernel, chips, factor, second_type),
        grid_spec=pltpu.PrefetchScalarGridSpec(
            num_scalar_prefetch=1,
            grid=(width // step,),
            in_specs=[pl.BlockSpec(piece.shape, lambda k, unused: (0, 0)), block, block, block, block, slot]
            + [pl.BlockSpec((part, step), lambda k, unused: (0, k)) for unused in weights],
            out_specs=[block, block, slot],
        ),
        out_shape=[
            pltpu.HBM((rows, width), F32),
            pltpu.HBM((rows, width), second_type),
            jax.ShapeDtypeStruct(grads.shape, BF16),
        ],
        input_output_aliases={6: 2},
        compiler_params=pltpu.CompilerParams(vmem_limit_bytes=VMEM_LIMIT),
        cost_estimate=pl.CostEstimate(
            flops=8 * rows * width * part,
            bytes_accessed=16 * rows * width,
            transcendentals=0,
        ),
    )(meta, piece, own, other, *totals, grads, *weights)


def core_swap(value):
    count = lax.axis_size("seq")
    return lax.ppermute(value, "seq", [(j, j ^ 1) for j in range(count)])


def chip_swap(value, delta):
    count = lax.axis_size("seq")
    return lax.ppermute(value, "seq", [(j, j ^ (2 * delta)) for j in range(count)])


def line_permutes(active):
    even = [pair for pair in active if min(pair) % 2 == 0]
    odd = [pair for pair in active if min(pair) % 2 == 1]
    return even, odd


def line_step(values, active):
    return [
        lax.ppermute(value, "head", pairs) if pairs else None
        for value, pairs in zip(values, line_permutes(active))
    ]


def line_sum(part_for, beside):
    count = lax.axis_size("head")
    mine = lax.axis_index("head")
    got = [None, None]
    for step in range(1, count):
        active = [(j, j + 1) for j in range(count - 1) if j <= step - 1]
        active += [(j, j - 1) for j in range(1, count) if count - 1 - j <= step - 1]
        values = []
        for parity, pairs in enumerate(line_permutes(active)):
            if not pairs:
                values.append(None)
                continue
            target = jnp.where(mine % 2 == parity, mine + count - step, mine - count + step)
            value = part_for(jnp.clip(target, 0, count - 1))
            if got[1 - parity] is not None:
                value = (value.astype(F32) + got[1 - parity].astype(F32)).astype(BF16)
            values.append(value)
        got = line_step(values, active)
        if beside.get(step):
            got, unused = lax.optimization_barrier((got, beside[step]))
    total = part_for(mine).astype(F32)
    for value in got:
        if value is not None:
            total = total + value.astype(F32)
    return total


def line_gather(value, tied):
    tied = dict(tied)
    count = lax.axis_size("head")
    mine = lax.axis_index("head")
    found, arrived = [(value, mine >= 0, mine)], {}
    got = [value, value]
    for step in range(1, count):
        active = [(j, j + 1) for j in range(count - 1) if j >= step - 1]
        active += [(j, j - 1) for j in range(1, count) if j + step - 1 <= count - 1]
        new = line_step([value if got[1 - q] is None else got[1 - q] for q in (0, 1)], active)
        if step in tied:
            new, tied[step] = lax.optimization_barrier((new, tied[step]))
        got = new
        arrived[step] = [item for item in got if item is not None]
        for parity, item in enumerate(got):
            if item is None:
                continue
            source = jnp.where(mine % 2 == parity, mine + step, mine - step)
            found.append((item, (source >= 0) & (source < count), source))
    return found, arrived, tied


def swapped_halves(total):
    core = lax.rem(lax.axis_index("seq"), 2)
    half_heads = total.shape[0] // 2
    mine = total.astype(BF16)
    other = core_swap(mine)
    both = mine.astype(F32) + other.astype(F32)
    half = lax.dynamic_slice_in_dim(both, core * half_heads, half_heads, 0).astype(BF16)
    return half, other


def sum_of_others(half, arrived, other, lower):
    position = lax.axis_index("seq")
    chip, core = lax.div(position, 2), lax.rem(position, 2)
    summed = jnp.zeros(half.shape, F32)
    for delta, item in enumerate(arrived, 1):
        partner = chip ^ delta
        counts = (partner < chip) if lower else (partner > chip)
        summed = summed + jnp.where(counts, item.astype(F32), 0.0)
    summed = summed.astype(BF16)
    swapped = core_swap(summed)
    first = jnp.where(core == 0, summed, swapped)
    second = jnp.where(core == 0, swapped, summed)
    whole = jnp.concatenate([first, second], axis=0).astype(F32)
    return whole + jnp.where(core == (1 if lower else 0), other.astype(F32), 0.0)


def near_pieces(own):
    chips = lax.axis_size("seq") // 2
    if chips != 4:
        pieces = [own] + [chip_swap(own, delta) for delta in range(1, chips)]
        return pieces[1:], lambda arrived: [own, *arrived]
    half = own.shape[0] // 2

    def rest(arrived):
        first = chip_swap(arrived[0][:half], 2)
        second = chip_swap(arrived[1][half:], 1)
        return [own, *arrived, jnp.concatenate([first, second], axis=0)]

    return [chip_swap(own, 1), chip_swap(own, 2)], rest


def scatter_start(grads):
    chips, part = grads.shape[:2]
    if chips != 4:
        sent = [chip_swap(grads[delta], delta) for delta in range(1, chips)]
        return sent, lambda arrived: (arrived, lambda final: added(grads[0], *final))
    half = part // 2
    upper, lower = slice(0, half), slice(half, part)
    sent = [chip_swap(grads[1::2, upper], 1), chip_swap(grads[2:, lower], 2)]

    def second(arrived):
        by_x, by_y = arrived
        upper_sum = added(grads[2, upper], by_x[1]).astype(BF16)
        lower_sum = added(grads[1, lower], by_y[1]).astype(BF16)

        def finish(final):
            return jnp.concatenate(
                [
                    added(grads[0, upper], by_x[0], final[0]),
                    added(grads[0, lower], by_y[0], final[1]),
                ],
                axis=0,
            )

        return [chip_swap(upper_sum, 2), chip_swap(lower_sum, 1)], finish

    return sent, second


def added(*values):
    return sum(value.astype(F32) for value in values)


def on_device(query_rows, key_rows, value_rows, out_weight, target_rows):
    rows, width = query_rows.shape
    heads = width // DH
    groups = lax.axis_size("head")
    seq_count = lax.axis_size("seq")
    chips = seq_count // 2
    share = chips // groups
    position = lax.axis_index("seq")
    chip, core = lax.div(position, 2), lax.rem(position, 2)
    held = out_weight.shape[0]
    chunks = CHUNKS if held % (CHUNKS * DH) == 0 else 1
    part = held // chunks
    call = functools.partial(per_head, rows=rows, heads=heads)
    barrier = lax.optimization_barrier
    outer = call(outer_kernel, ins="hh", outs=[("m", F32)], macs=rows * DH * DH, step=4)

    positions = (position * rows + jnp.arange(rows, dtype=jnp.int32) + 1).astype(F32)
    scale = lax.rsqrt(F32(DH) * positions)[:, None]
    (key_value,) = outer(key_rows, value_rows)
    half, other = swapped_halves(key_value)
    half, query_rows = barrier((half, query_rows))
    arrived = [chip_swap(half, delta) for delta in range(1, chips)]
    near, rest = near_pieces(out_weight[:part])
    scaled, intra = call(
        forward_kernel, ins="hhhs", outs=[("h", BF16), ("h", F32)], macs=2 * rows * rows * DH
    )(query_rows, key_rows, value_rows, scale)
    near, scaled, intra = barrier((near, scaled, intra))
    pieces = rest(near)
    arrived, scaled = barrier((arrived, scaled))
    before = sum_of_others(half, arrived, other, True)
    (attended,) = call(
        attended_kernel, ins="hhm", outs=[("h", BF16)], macs=2 * rows * DH * DH, step=4
    )(scaled, intra, before)
    attended, pieces, target_rows = barrier((attended, pieces, target_rows))
    other_attended = core_swap(attended)

    def features_of(array, group, first, count):
        found = [
            lax.dynamic_slice_in_dim(array, (2 * j + group) * held + first, count, 1)
            for j in range(share)
        ]
        return found[0] if share == 1 else jnp.concatenate(found, axis=1)

    def chunk_of(array, c):
        found = [array[:, j * held + c * part : j * held + (c + 1) * part] for j in range(share)]
        return found[0] if share == 1 else jnp.concatenate(found, axis=1)

    other_targets = core_swap(features_of(target_rows, 1 - core, 0, held))
    targets = [
        jnp.concatenate(
            [features_of(target_rows, core, c * part, part), chunk_of(other_targets, c)], axis=0
        )
        for c in range(chunks)
    ]

    outputs, grad_parts = [], []
    gate, totals, sent, pending, gathered = None, (), None, None, {}
    factor = 1.0 / math.sqrt(rows * seq_count)
    for c in range(chunks):
        last = c == chunks - 1
        if c:
            own_rows, unused = barrier((out_weight, pieces[-1]))
            near, rest = near_pieces(own_rows[c * part : (c + 1) * part])
            pieces = rest(near)
        partial_out = project(attended, other_attended, pieces)
        if gate is not None:
            partial_out, gate, outputs[-1] = barrier((partial_out, gate, outputs[-1]))

        def part_for(group, partial_out=partial_out):
            found = [
                lax.dynamic_index_in_dim(partial_out, (group * share + j) ^ chip, 0, keepdims=False)
                for j in range(share)
            ]
            return found[0] if share == 1 else jnp.concatenate(found, axis=1)

        summed = line_sum(part_for, {step - 1: items for step, items in gathered.items() if step > 1}).astype(BF16)
        residual = (summed.astype(F32) - targets[c].astype(F32)).astype(BF16)
        own_output = summed[:rows]
        other_output = core_swap(summed[rows:])
        outputs.append(
            [
                jnp.where(core == 0, own_output, other_output),
                jnp.where(core == 0, other_output, own_output),
            ]
        )
        output = None
        if last:
            output = jnp.concatenate(
                [
                    piece[group][:, j * part : (j + 1) * part]
                    for j in range(share)
                    for group in (0, 1)
                    for piece in outputs
                ],
                axis=1,
            )
        if pending is not None:
            pending, output = barrier((pending, output))
            sent, second_step = scatter_start(pending)
        found, gathered, tied = line_gather(
            residual, {1: totals, 2: output}
        )
        totals, output = tied[1], tied[2]
        gate = residual
        weights = pieces
        on_time = found[:-1] if last and len(found) > 1 else found
        metas = [
            [
                value
                for j in range(share)
                for value in (
                    valid.astype(jnp.int32),
                    jnp.clip((source * share + j) ^ chip, 0, chips - 1).astype(jnp.int32),
                )
            ]
            for unused, valid, source in found
        ]
        late = found[len(on_time) :]
        if not last:
            items = [item for item, unused, unused in on_time]
            if sent is not None:
                sent, finish = second_step(sent)
                items, sent = barrier((items, sent))
                grad_parts.append(finish(sent))
        else:
            items = [item for item, unused, unused in on_time]
        *totals, grads = products(
            jnp.stack(sum(metas, [])),
            items,
            len(late) * share,
            attended,
            other_attended,
            weights,
            totals,
            factor,
        )
        if late:
            item = late[0][0]
            if sent is not None:
                sent, finish = second_step(sent)
                item, sent, totals = barrier((item, sent, totals))
                grad_parts.append(finish(sent))
            for j in range(share):
                *totals, grads = late_products(
                    jnp.stack(metas[-1][2 * j : 2 * j + 2]),
                    item[:, j * part : (j + 1) * part] if share > 1 else item,
                    attended,
                    other_attended,
                    weights,
                    totals,
                    grads,
                    BF16 if j == share - 1 else F32,
                    factor,
                )
        pending = grads

    sent, second_step = scatter_start(pending)
    grad_attended = (totals[0] + core_swap(totals[1]).astype(F32)).astype(BF16)
    (query_grad,) = call(outer_kernel, ins="vv", outs=[("m", F32)], macs=rows * DH * DH, step=4)(
        scaled, grad_attended
    )
    half, other = swapped_halves(query_grad)
    arrived = [chip_swap(half, delta) for delta in range(1, chips)]
    grad_query, key_part, value_part = call(
        backward_kernel,
        ins="vvvvsm",
        outs=[("h", BF16), ("v", F32), ("v", F32)],
        macs=5 * rows * rows * DH,
    )(scaled, key_rows, value_rows, grad_attended, scale, before)
    arrived, key_part, value_part, grad_query, sent = barrier(
        (arrived, key_part, value_part, grad_query, sent)
    )
    sent, finish = second_step(sent)
    after = sum_of_others(half, arrived, other, False)
    grad_key, grad_value = call(
        finish_kernel, ins="vvvvm", outs=[("h", BF16), ("h", BF16)], macs=4 * rows * DH * DH
    )(key_rows, value_rows, key_part, value_part, after)
    sent, grad_key, grad_value = barrier((sent, grad_key, grad_value))
    grad_weight = jnp.concatenate([*grad_parts, finish(sent)], axis=0)
    return output, grad_query, grad_key, grad_value, grad_weight


def solution(mesh):
    placed = P("seq", "head")
    return jax.shard_map(
        on_device,
        mesh=mesh,
        in_specs=(placed,) * 5,
        out_specs=(placed,) * 5,
        check_vma=False,
    )
```

```python
import functools
import math

import jax
import jax.numpy as jnp
from jax import lax
from jax.experimental import pallas as pl
from jax.experimental.pallas import tpu as pltpu
from jax.sharding import PartitionSpec as P

DH = 128
CHUNKS = 2
F32 = jnp.float32
BF16 = jnp.bfloat16
VMEM_LIMIT = 12 * 1024 * 1024

NT = (((1,), (1,)), ((), ()))
TN = (((0,), (0,)), ((), ()))
NN = (((1,), (0,)), ((), ()))


def in_hbm(values):
    return [pltpu.with_memory_space_constraint(value, pltpu.HBM) for value in values]


def dot(a, b, dims):
    return lax.dot_general(a, b, dims, preferred_element_type=F32)


def split_dot(a, state, dims):
    high = state.astype(BF16)
    low = (state - high.astype(F32)).astype(BF16)
    return dot(a, high, dims) + dot(a, low, dims)


def head_columns(ref):
    return [ref.at[:, h * DH : (h + 1) * DH] for h in range(ref.shape[1] // DH)]


def outer_kernel(a_ref, b_ref, out_ref):
    for h, (a, b) in enumerate(zip(head_columns(a_ref), head_columns(b_ref))):
        out_ref[h] = dot(a[...], b[...], TN)


def halves(rows):
    middle = rows // 2
    return [(slice(0, middle), slice(0, middle)), (slice(middle, rows), slice(0, rows))]


def masked(product):
    rows, columns = product.shape
    t = lax.broadcasted_iota(jnp.int32, product.shape, 0) + (columns - rows)
    s = lax.broadcasted_iota(jnp.int32, product.shape, 1)
    return jnp.where(s <= t, product, 0.0).astype(BF16)


def forward_kernel(q_ref, k_ref, v_ref, scale_ref, scaled_ref, intra_ref):
    scaled_ref[...] = (q_ref[...].astype(F32) * scale_ref[...]).astype(BF16)
    refs = (scaled_ref, k_ref, v_ref, intra_ref)
    for scaled, keys, values, intra in zip(*map(head_columns, refs)):
        for own, upto in halves(scaled_ref.shape[0]):
            scores = masked(dot(scaled[own], keys[upto], NT))
            intra[own] = dot(scores, values[upto], NN)


def attended_kernel(scaled_ref, intra_ref, state_ref, out_ref):
    refs = (scaled_ref, intra_ref, out_ref)
    for h, (scaled, intra, out) in enumerate(zip(*map(head_columns, refs))):
        out[...] = (split_dot(scaled[...], state_ref[h], NN) + intra[...]).astype(BF16)


def backward_kernel(
    scaled_ref, k_ref, v_ref, g_ref, scale_ref, state_ref, dq_ref, dk_ref, dv_ref
):
    rows = scaled_ref.shape[0]
    refs = (scaled_ref, k_ref, v_ref, g_ref, dq_ref, dk_ref, dv_ref)
    for h, (scaled, keys, values, grads, dq, dk, dv) in enumerate(zip(*map(head_columns, refs))):
        inter = split_dot(grads[...], state_ref[h], NT)
        for own, upto in reversed(halves(rows)):
            mixed = masked(dot(grads[own], values[upto], NT))
            scores = masked(dot(scaled[own], keys[upto], NT))
            total = inter[own] + dot(mixed, keys[upto], NN)
            dq[own] = (total * scale_ref[own]).astype(BF16)
            key_part = dot(mixed, scaled[own], TN)
            value_part = dot(scores, grads[own], TN)
            if upto.stop == rows:
                dk[...] = key_part
                dv[...] = value_part
            else:
                dk[upto] += key_part
                dv[upto] += value_part


def finish_kernel(k_ref, v_ref, dk_part_ref, dv_part_ref, after_ref, dk_ref, dv_ref):
    refs = (k_ref, v_ref, dk_part_ref, dv_part_ref, dk_ref, dv_ref)
    for h, (keys, values, dk_part, dv_part, dk, dv) in enumerate(zip(*map(head_columns, refs))):
        dk[...] = (split_dot(values[...], after_ref[h], NT) + dk_part[...]).astype(BF16)
        dv[...] = (split_dot(keys[...], after_ref[h], NN) + dv_part[...]).astype(BF16)


def per_head(kernel, rows, heads, ins, outs, macs, step=2):
    if heads % step:
        step = 1
    specs = {
        "h": pl.BlockSpec((rows, step * DH), lambda h: (0, h)),
        "v": pl.BlockSpec((rows, step * DH), lambda h: (0, h)),
        "m": pl.BlockSpec((step, DH, DH), lambda h: (h, 0, 0)),
        "s": pl.BlockSpec((rows, 1), lambda h: (0, 0)),
    }
    shapes = {"h": (rows, heads * DH), "v": (rows, heads * DH), "m": (heads, DH, DH)}
    call = pl.pallas_call(
        kernel,
        grid=(heads // step,),
        in_specs=[specs[kind] for kind in ins],
        out_specs=[specs[kind] for kind, unused in outs],
        out_shape=[
            (pltpu.HBM if kind == "h" else jax.ShapeDtypeStruct)(shapes[kind], dtype)
            for kind, dtype in outs
        ],
        compiler_params=pltpu.CompilerParams(vmem_limit_bytes=VMEM_LIMIT),
        cost_estimate=pl.CostEstimate(
            flops=2 * macs * heads,
            bytes_accessed=rows * heads * DH * 2 * (len(ins) + len(outs)),
            transcendentals=0,
        ),
    )

    def on_values(*values):
        return call(
            *[in_hbm([value])[0] if kind == "h" else value for kind, value in zip(ins, values)]
        )

    return on_values


def project_kernel(pieces, a_ref, *refs):
    for piece in range(pieces):
        refs[-1][piece] = dot(a_ref[...], refs[piece][...], NT).astype(BF16)


def project_rows(attended, pieces, half, into):
    rows, width = attended.shape
    features = pieces[0].shape[0]
    step = min(rows, 256)
    first = half * (rows // step)
    more = [] if into is None else [into]
    return pl.pallas_call(
        functools.partial(project_kernel, len(pieces)),
        grid=(rows // step,),
        in_specs=[pl.BlockSpec((step, width), lambda r: (r, 0))]
        + [pl.BlockSpec((features, width), lambda r: (0, 0)) for unused in pieces]
        + [pl.BlockSpec(memory_space=pl.ANY) for unused in more],
        out_specs=pl.BlockSpec((len(pieces), step, features), lambda r: (0, r + first, 0)),
        out_shape=jax.ShapeDtypeStruct((len(pieces), 2 * rows, features), BF16),
        input_output_aliases={len(pieces) + 1: 0} if more else {},
        compiler_params=pltpu.CompilerParams(vmem_limit_bytes=VMEM_LIMIT),
        cost_estimate=pl.CostEstimate(
            flops=2 * rows * width * features * len(pieces),
            bytes_accessed=4 * rows * width,
            transcendentals=0,
        ),
    )(*([attended] if more else in_hbm([attended])), *in_hbm(pieces), *more)


def project(own, other, pieces):
    return project_rows(other, pieces, 1, project_rows(own, pieces, 0, None))


def products_kernel(count, late, chips, before, factor, meta_ref, *refs):
    candidates, (own_ref, other_ref), rest = refs[:count], refs[count : count + 2], refs[count + 2 :]
    weights, rest = rest[:chips], rest[chips:]
    earlier, rest = rest[:before], rest[before:]
    first_ref, second_ref, grad_ref, gathered, turned, semaphores = rest
    rows = own_ref.shape[0]
    part = weights[0].shape[0]

    @pl.when(pl.program_id(0) == 0)
    def unused():
        copies = []
        for j, candidate in enumerate(candidates):
            for u in range(candidate.shape[1] // part):
                copies.append(
                    (
                        meta_ref[2 * len(copies)] == 1,
                        pltpu.make_async_copy(
                            candidate.at[:, u * part : (u + 1) * part],
                            gathered.at[meta_ref[2 * len(copies) + 1]],
                            semaphores.at[len(copies)],
                        ),
                    )
                )
        for valid, copy in copies:
            pl.when(valid)(copy.start)
        for j in range(len(copies), len(copies) + late):

            @pl.when(meta_ref[2 * j] == 1)
            def unused_zero(j=j):
                gathered[meta_ref[2 * j + 1]] = jnp.zeros(gathered.shape[1:], BF16)

        for valid, copy in copies:
            pl.when(valid)(copy.wait)
        for delta in range(chips):
            turned[delta * part : (delta + 1) * part, :] = gathered[delta].T

    residuals = jnp.concatenate([gathered[delta] for delta in range(chips)], axis=1)
    weight = jnp.concatenate([piece[...] for piece in weights], axis=0)
    total = dot(residuals, weight, NN)
    first, second = total[:rows], total[rows:]
    if before:
        first, second = first + earlier[0][...], second + earlier[1][...]
    first_ref[...] = first
    second_ref[...] = second
    grad = dot(turned[:, :rows], own_ref[...], NN) + dot(turned[:, rows:], other_ref[...], NN)
    grad = (grad * factor).astype(BF16)
    for delta in range(chips):
        grad_ref[delta] = grad[delta * part : (delta + 1) * part]


def products(meta, candidates, late, own, other, weights, earlier, factor):
    rows, width = own.shape
    chips, part = len(weights), weights[0].shape[0]
    step = 256 if width % 256 == 0 else DH
    block = pl.BlockSpec((rows, step), lambda k, unused: (0, k))
    pieces = pl.BlockSpec((chips, part, step), lambda k, unused: (0, 0, k))
    place = jax.ShapeDtypeStruct if late else pltpu.HBM
    copies = sum(c.shape[1] for c in candidates) // part
    return pl.pallas_call(
        functools.partial(products_kernel, len(candidates), late, chips, len(earlier), factor),
        grid_spec=pltpu.PrefetchScalarGridSpec(
            num_scalar_prefetch=1,
            grid=(width // step,),
            in_specs=[pl.BlockSpec(memory_space=pltpu.HBM) for unused in candidates]
            + [block, block]
            + [pl.BlockSpec((part, step), lambda k, unused: (0, k)) for unused in weights]
            + [block for unused in earlier],
            out_specs=[block, block, pieces],
            scratch_shapes=[
                pltpu.VMEM((chips, 2 * rows, part), BF16),
                pltpu.VMEM((chips * part, 2 * rows), BF16),
                pltpu.SemaphoreType.DMA((copies,)),
            ],
        ),
        out_shape=[
            place((rows, width), F32),
            place((rows, width), F32),
            place((chips, part, width), BF16),
        ],
        compiler_params=pltpu.CompilerParams(vmem_limit_bytes=24 * rows * chips * part),
        cost_estimate=pl.CostEstimate(
            flops=8 * rows * width * part * chips,
            bytes_accessed=16 * rows * width,
            transcendentals=0,
        ),
    )(meta, *in_hbm([*candidates, own, other, *weights, *earlier]))


def late_kernel(
    chips, factor, second_type, meta_ref, piece_ref, own_ref, other_ref, first_in, second_in, grad_in, *refs
):
    weights, (first_ref, second_ref, grad_ref) = refs[:chips], refs[chips:]
    rows = own_ref.shape[0]
    valid, place = meta_ref[0] == 1, meta_ref[1]

    @pl.when(jnp.logical_not(valid))
    def unused_pass():
        first_ref[...] = first_in[...]
        second_ref[...] = second_in[...].astype(second_type)
        grad_ref[...] = grad_in[...]

    for delta, weight in enumerate(weights):

        @pl.when(valid & (place == delta))
        def unused_add(weight=weight):
            total = dot(piece_ref[...], weight[...], NN)
            first_ref[...] = first_in[...] + total[:rows]
            second_ref[...] = (second_in[...] + total[rows:]).astype(second_type)

    @pl.when(valid)
    def unused_grad():
        grad = dot(piece_ref[:rows], own_ref[...], TN) + dot(piece_ref[rows:], other_ref[...], TN)
        grad_ref[0] = (grad * factor).astype(BF16)


def late_products(meta, piece, own, other, weights, totals, grads, second_type, factor):
    rows, width = own.shape
    chips, part = len(weights), weights[0].shape[0]
    step = min(width, 512)
    block = pl.BlockSpec((rows, step), lambda k, unused: (0, k))
    slot = pl.BlockSpec((1, part, step), lambda k, meta: (meta[1], 0, k))
    return pl.pallas_call(
        functools.partial(late_kernel, chips, factor, second_type),
        grid_spec=pltpu.PrefetchScalarGridSpec(
            num_scalar_prefetch=1,
            grid=(width // step,),
            in_specs=[pl.BlockSpec(piece.shape, lambda k, unused: (0, 0)), block, block, block, block, slot]
            + [pl.BlockSpec((part, step), lambda k, unused: (0, k)) for unused in weights],
            out_specs=[block, block, slot],
        ),
        out_shape=[
            pltpu.HBM((rows, width), F32),
            pltpu.HBM((rows, width), second_type),
            jax.ShapeDtypeStruct(grads.shape, BF16),
        ],
        input_output_aliases={6: 2},
        compiler_params=pltpu.CompilerParams(vmem_limit_bytes=VMEM_LIMIT),
        cost_estimate=pl.CostEstimate(
            flops=8 * rows * width * part,
            bytes_accessed=16 * rows * width,
            transcendentals=0,
        ),
    )(meta, piece, own, other, *totals, grads, *weights)


def core_swap(value):
    count = lax.axis_size("seq")
    return lax.ppermute(value, "seq", [(j, j ^ 1) for j in range(count)])


def chip_swap(value, delta):
    count = lax.axis_size("seq")
    return lax.ppermute(value, "seq", [(j, j ^ (2 * delta)) for j in range(count)])


def line_permutes(active):
    even = [pair for pair in active if min(pair) % 2 == 0]
    odd = [pair for pair in active if min(pair) % 2 == 1]
    return even, odd


def line_step(values, active):
    return [
        lax.ppermute(value, "head", pairs) if pairs else None
        for value, pairs in zip(values, line_permutes(active))
    ]


def line_sum(part_for, beside):
    count = lax.axis_size("head")
    mine = lax.axis_index("head")
    got = [None, None]
    for step in range(1, count):
        active = [(j, j + 1) for j in range(count - 1) if j <= step - 1]
        active += [(j, j - 1) for j in range(1, count) if count - 1 - j <= step - 1]
        values = []
        for parity, pairs in enumerate(line_permutes(active)):
            if not pairs:
                values.append(None)
                continue
            target = jnp.where(mine % 2 == parity, mine + count - step, mine - count + step)
            value = part_for(jnp.clip(target, 0, count - 1))
            if got[1 - parity] is not None:
                value = (value.astype(F32) + got[1 - parity].astype(F32)).astype(BF16)
            values.append(value)
        got = line_step(values, active)
        if beside.get(step):
            got, unused = lax.optimization_barrier((got, beside[step]))
    total = part_for(mine).astype(F32)
    for value in got:
        if value is not None:
            total = total + value.astype(F32)
    return total


def line_gather(value, tied):
    tied = dict(tied)
    count = lax.axis_size("head")
    mine = lax.axis_index("head")
    found, arrived = [(value, mine >= 0, mine)], {}
    got = [value, value]
    for step in range(1, count):
        active = [(j, j + 1) for j in range(count - 1) if j >= step - 1]
        active += [(j, j - 1) for j in range(1, count) if j + step - 1 <= count - 1]
        new = line_step([value if got[1 - q] is None else got[1 - q] for q in (0, 1)], active)
        if step in tied:
            new, tied[step] = lax.optimization_barrier((new, tied[step]))
        got = new
        arrived[step] = [item for item in got if item is not None]
        for parity, item in enumerate(got):
            if item is None:
                continue
            source = jnp.where(mine % 2 == parity, mine + step, mine - step)
            found.append((item, (source >= 0) & (source < count), source))
    return found, arrived, tied


def swapped_halves(total):
    core = lax.rem(lax.axis_index("seq"), 2)
    half_heads = total.shape[0] // 2
    mine = total.astype(BF16)
    other = core_swap(mine)
    both = mine.astype(F32) + other.astype(F32)
    half = lax.dynamic_slice_in_dim(both, core * half_heads, half_heads, 0).astype(BF16)
    return half, other


def sum_of_others(half, arrived, other, lower):
    position = lax.axis_index("seq")
    chip, core = lax.div(position, 2), lax.rem(position, 2)
    summed = jnp.zeros(half.shape, F32)
    for delta, item in enumerate(arrived, 1):
        partner = chip ^ delta
        counts = (partner < chip) if lower else (partner > chip)
        summed = summed + jnp.where(counts, item.astype(F32), 0.0)
    summed = summed.astype(BF16)
    swapped = core_swap(summed)
    first = jnp.where(core == 0, summed, swapped)
    second = jnp.where(core == 0, swapped, summed)
    whole = jnp.concatenate([first, second], axis=0).astype(F32)
    return whole + jnp.where(core == (1 if lower else 0), other.astype(F32), 0.0)


def near_pieces(own):
    chips = lax.axis_size("seq") // 2
    if chips != 4:
        pieces = [own] + [chip_swap(own, delta) for delta in range(1, chips)]
        return pieces[1:], lambda arrived: [own, *arrived]
    half = own.shape[0] // 2

    def rest(arrived):
        first = chip_swap(arrived[0][:half], 2)
        second = chip_swap(arrived[1][half:], 1)
        return [own, *arrived, jnp.concatenate([first, second], axis=0)]

    return [chip_swap(own, 1), chip_swap(own, 2)], rest


def scatter_start(grads):
    chips, part = grads.shape[:2]
    if chips != 4:
        sent = [chip_swap(grads[delta], delta) for delta in range(1, chips)]
        return sent, lambda arrived: (arrived, lambda final: added(grads[0], *final))
    half = part // 2
    upper, lower = slice(0, half), slice(half, part)
    sent = [chip_swap(grads[1::2, upper], 1), chip_swap(grads[2:, lower], 2)]

    def second(arrived):
        by_x, by_y = arrived
        upper_sum = added(grads[2, upper], by_x[1]).astype(BF16)
        lower_sum = added(grads[1, lower], by_y[1]).astype(BF16)

        def finish(final):
            return jnp.concatenate(
                [
                    added(grads[0, upper], by_x[0], final[0]),
                    added(grads[0, lower], by_y[0], final[1]),
                ],
                axis=0,
            )

        return [chip_swap(upper_sum, 2), chip_swap(lower_sum, 1)], finish

    return sent, second


def added(*values):
    return sum(value.astype(F32) for value in values)


def on_device(query_rows, key_rows, value_rows, out_weight, target_rows):
    rows, width = query_rows.shape
    heads = width // DH
    groups = lax.axis_size("head")
    seq_count = lax.axis_size("seq")
    chips = seq_count // 2
    share = chips // groups
    position = lax.axis_index("seq")
    chip, core = lax.div(position, 2), lax.rem(position, 2)
    held = out_weight.shape[0]
    chunks = CHUNKS if held % (CHUNKS * DH) == 0 else 1
    part = held // chunks
    call = functools.partial(per_head, rows=rows, heads=heads)
    barrier = lax.optimization_barrier
    outer = call(outer_kernel, ins="hh", outs=[("m", F32)], macs=rows * DH * DH, step=4)

    positions = (position * rows + jnp.arange(rows, dtype=jnp.int32) + 1).astype(F32)
    scale = lax.rsqrt(F32(DH) * positions)[:, None]
    (key_value,) = outer(key_rows, value_rows)
    half, other = swapped_halves(key_value)
    half, query_rows = barrier((half, query_rows))
    arrived = [chip_swap(half, delta) for delta in range(1, chips)]
    near, rest = near_pieces(out_weight[:part])
    scaled, intra = call(
        forward_kernel, ins="hhhs", outs=[("h", BF16), ("h", F32)], macs=2 * rows * rows * DH
    )(query_rows, key_rows, value_rows, scale)
    near, scaled, intra = barrier((near, scaled, intra))
    pieces = rest(near)
    arrived, scaled = barrier((arrived, scaled))
    before = sum_of_others(half, arrived, other, True)
    (attended,) = call(
        attended_kernel, ins="hhm", outs=[("h", BF16)], macs=2 * rows * DH * DH, step=4
    )(scaled, intra, before)
    attended, pieces, target_rows = barrier((attended, pieces, target_rows))
    other_attended = core_swap(attended)

    def features_of(array, group, first, count):
        found = [
            lax.dynamic_slice_in_dim(array, (2 * j + group) * held + first, count, 1)
            for j in range(share)
        ]
        return found[0] if share == 1 else jnp.concatenate(found, axis=1)

    def chunk_of(array, c):
        found = [array[:, j * held + c * part : j * held + (c + 1) * part] for j in range(share)]
        return found[0] if share == 1 else jnp.concatenate(found, axis=1)

    other_targets = core_swap(features_of(target_rows, 1 - core, 0, held))
    targets = [
        jnp.concatenate(
            [features_of(target_rows, core, c * part, part), chunk_of(other_targets, c)], axis=0
        )
        for c in range(chunks)
    ]

    outputs, grad_parts = [], []
    gate, totals, sent, pending, gathered = None, (), None, None, {}
    factor = 1.0 / math.sqrt(rows * seq_count)
    for c in range(chunks):
        last = c == chunks - 1
        if c:
            own_rows, unused = barrier((out_weight, pieces[-1]))
            near, rest = near_pieces(own_rows[c * part : (c + 1) * part])
            pieces = rest(near)
        partial_out = project(attended, other_attended, pieces)
        if gate is not None:
            partial_out, gate, outputs[-1] = barrier((partial_out, gate, outputs[-1]))

        def part_for(group, partial_out=partial_out):
            found = [
                lax.dynamic_index_in_dim(partial_out, (group * share + j) ^ chip, 0, keepdims=False)
                for j in range(share)
            ]
            return found[0] if share == 1 else jnp.concatenate(found, axis=1)

        summed = line_sum(part_for, {step - 1: items for step, items in gathered.items() if step > 1}).astype(BF16)
        residual = (summed.astype(F32) - targets[c].astype(F32)).astype(BF16)
        own_output = summed[:rows]
        other_output = core_swap(summed[rows:])
        outputs.append(
            [
                jnp.where(core == 0, own_output, other_output),
                jnp.where(core == 0, other_output, own_output),
            ]
        )
        output = None
        if last:
            output = jnp.concatenate(
                [
                    piece[group][:, j * part : (j + 1) * part]
                    for j in range(share)
                    for group in (0, 1)
                    for piece in outputs
                ],
                axis=1,
            )
        if pending is not None:
            pending, output = barrier((pending, output))
            sent, second_step = scatter_start(pending)
        found, gathered, tied = line_gather(
            residual, {1: totals, 2: output}
        )
        totals, output = tied[1], tied[2]
        gate = residual
        weights = pieces
        on_time = found[:-1] if last and len(found) > 1 else found
        metas = [
            [
                value
                for j in range(share)
                for value in (
                    valid.astype(jnp.int32),
                    jnp.clip((source * share + j) ^ chip, 0, chips - 1).astype(jnp.int32),
                )
            ]
            for unused, valid, source in found
        ]
        late = found[len(on_time) :]
        if not last:
            items = [item for item, unused, unused in on_time]
            if sent is not None:
                sent, finish = second_step(sent)
                items, sent = barrier((items, sent))
                grad_parts.append(finish(sent))
        else:
            items = [item for item, unused, unused in on_time]
        *totals, grads = products(
            jnp.stack(sum(metas, [])),
            items,
            len(late) * share,
            attended,
            other_attended,
            weights,
            totals,
            factor,
        )
        if late:
            item = late[0][0]
            if sent is not None:
                sent, finish = second_step(sent)
                item, sent, totals = barrier((item, sent, totals))
                grad_parts.append(finish(sent))
            for j in range(share):
                *totals, grads = late_products(
                    jnp.stack(metas[-1][2 * j : 2 * j + 2]),
                    item[:, j * part : (j + 1) * part] if share > 1 else item,
                    attended,
                    other_attended,
                    weights,
                    totals,
                    grads,
                    BF16 if j == share - 1 else F32,
                    factor,
                )
        pending = grads

    sent, second_step = scatter_start(pending)
    grad_attended = (totals[0] + core_swap(totals[1]).astype(F32)).astype(BF16)
    (query_grad,) = call(outer_kernel, ins="vv", outs=[("m", F32)], macs=rows * DH * DH, step=4)(
        scaled, grad_attended
    )
    half, other = swapped_halves(query_grad)
    arrived = [chip_swap(half, delta) for delta in range(1, chips)]
    grad_query, key_part, value_part = call(
        backward_kernel,
        ins="vvvvsm",
        outs=[("h", BF16), ("v", F32), ("v", F32)],
        macs=5 * rows * rows * DH,
    )(scaled, key_rows, value_rows, grad_attended, scale, before)
    arrived, key_part, value_part, grad_query, sent = barrier(
        (arrived, key_part, value_part, grad_query, sent)
    )
    sent, finish = second_step(sent)
    after = sum_of_others(half, arrived, other, False)
    grad_key, grad_value = call(
        finish_kernel, ins="vvvvm", outs=[("h", BF16), ("h", BF16)], macs=4 * rows * DH * DH, step=4
    )(key_rows, value_rows, key_part, value_part, after)
    sent, grad_key, grad_value = barrier((sent, grad_key, grad_value))
    grad_weight = jnp.concatenate([*grad_parts, finish(sent)], axis=0)
    return output, grad_query, grad_key, grad_value, grad_weight


def solution(mesh):
    placed = P("seq", "head")
    return jax.shard_map(
        on_device,
        mesh=mesh,
        in_specs=(placed,) * 5,
        out_specs=(placed,) * 5,
        check_vma=False,
    )
```
